32 devices in a mesh: row: 8 (over z, core), col: 4 (over y, x).
Axes of the slice: x: 2, y: 2, z: 4, core: 2. Of those that a mesh axis runs over, the one named last changes fastest.
Arguments:
- inputs: bfloat16 [512, 8192], P('col', 'row'), may hold values from -6 to 6
- weight: bfloat16 [8192, 28672], P('row', 'col'), may hold values from -0.09375 to 0.09375
- mask: int32 [64, 224], P('row', 'col'), may hold values 0 or 1
- cotangent: bfloat16 [512, 28672], P('row', 'col'), may hold values from -6 to 6
Outputs:
- outputs: bfloat16 [512, 28672], P('row', 'col')
- input_grad: bfloat16 [512, 8192], P('col', 'row')
- weight_grad: bfloat16 [8192, 28672], P('row', 'col')
The draws below stay inside these ranges and needn't reach their ends.
Inputs may be any that keep to these rules, and one draw needn't show every extreme that they name: mask holds only zeros and ones.
All inputs are finite; a program needn't handle non-finite values. No bound on the sum of `mask` on one device may be relied on, other than what follows from the above.
Results may differ from the reference program's by a relative error of at most 0.022.
Values may be sent and summed in bfloat16 or wider, within the bound.
No kernel may reach another device: no remote copies, remote signals or barrier semaphores. Data moves between devices by JAX's collectives and lax.ppermute only.
A program may use at most 128 MiB of HBM per device.

```python
import jax
import jax.numpy as jnp
from jax import lax

D = 8192
F = 28672
BLOCK = 128
TOKENS = 512
N_ROW = 8
N_COL = 4


def plant(entries, own_key, smallest, largest):
    dims = entries.shape
    index_at = [jax.random.randint(jax.random.fold_in(own_key, axis), (), 0, dims[axis]) for axis in range(len(dims))]
    entries = entries.at[tuple(index_at)].set(smallest)
    longest = dims.index(max(dims))
    index_at[longest] = (index_at[longest] + 1) % dims[longest]
    return entries.at[tuple(index_at)].set(largest)


def spiked(result, stream_key, source, target, shards_of, factor):
    def block_of(dim):
        return (jnp.arange(result.shape[dim]) // (result.shape[dim] // shards_of)).reshape((-1,) + (1,) * (result.ndim - 1 - dim))

    near = jax.random.permutation(stream_key, shards_of)[block_of(target)]
    far = (block_of(target) + shards_of // 2) % shards_of
    return jnp.where((block_of(source) == near) | (block_of(source) == far), factor * result, result)


def level_of(stream_key, dims, shards, smallest, high):
    level = 1.0
    for position, blocks in shards:
        heights = jax.random.uniform(jax.random.fold_in(jax.random.fold_in(stream_key, 6), position), (blocks,), jnp.float32, smallest / len(shards), high / len(shards))
        level = level * jnp.repeat(jnp.exp(heights), dims[position] // blocks).reshape((-1,) + (1,) * (len(dims) - 1 - position))
    return level


def bell_draw(key, dims, deviation, bound, pieces=(), kind=jnp.bfloat16):
    level = level_of(key, dims, pieces, -0.22, 0.18) if pieces else 1.0
    array = jax.random.normal(key, dims, jnp.float32) * deviation * level
    return jnp.minimum(jnp.maximum(array, -bound), bound).astype(kind)


def bell_draw_with(stream_key, extent, spread, reach, cuts, heavy, held_as=jnp.bfloat16):
    result = spread * jax.random.normal(stream_key, extent, jnp.float32)
    if cuts:
        result = result * level_of(stream_key, extent, cuts, -0.22, 0.18)
    return jnp.clip(spiked(result, jax.random.fold_in(stream_key, 3), *heavy), -reach, reach).astype(held_as)


def setup_inputs(seed: int = 0) -> dict:
    splits = jax.random.split(jax.random.key(seed), 5)
    return {
        "inputs": bell_draw_with(splits[0], (TOKENS, D), 1.0, 6.0, ((0, 4), (1, 8)), (1, 0, 8, 2.0)),
        "weight": bell_draw(splits[1], (D, F), (D // 2) ** -0.5, 0.09375, ((0, 8), (1, 4))),
        "mask": plant((jax.random.randint(splits[2], (D // BLOCK, F // BLOCK), 0, 2) < 1).astype(jnp.int32), jax.random.fold_in(splits[2], 1), 0, 1),
        "cotangent": bell_draw_with(splits[3], (TOKENS, F), 1.0, 6.0, ((0, 8), (1, 4)), (1, 0, 8, 2.0)),
    }


def expand_mask(mask_tile):
    tile_rows, tile_cols = mask_tile.shape
    mask_float = mask_tile.astype(jnp.float32)
    widened = jnp.broadcast_to(mask_float[:, None, :, None], (tile_rows, BLOCK, tile_cols, BLOCK))
    return widened.reshape(tile_rows * BLOCK, tile_cols * BLOCK)


def rounded(value):
    return lax.optimization_barrier(value.astype(jnp.bfloat16)).astype(jnp.float32)


def reference(inputs, weight, mask, cotangent):
    keep_mask = expand_mask(mask)
    masked = (weight.astype(jnp.float32) * keep_mask).astype(jnp.bfloat16)
    row_width = D // N_ROW
    col_width = F // N_COL
    forward_acc = jnp.zeros((TOKENS, F), jnp.float32)
    for row_index in range(N_ROW):
        lower_edge = row_index * row_width
        upper_edge = lower_edge + row_width
        partial_value = jnp.dot(inputs[:, lower_edge:upper_edge], masked[lower_edge:upper_edge, :], preferred_element_type=jnp.float32)
        forward_acc = forward_acc + rounded(partial_value)
    outputs = forward_acc.astype(jnp.bfloat16)
    grad_acc = jnp.zeros((TOKENS, D), jnp.float32)
    for col_index in range(N_COL):
        lower_edge = col_index * col_width
        upper_edge = lower_edge + col_width
        partial_value = lax.dot_general(cotangent[:, lower_edge:upper_edge], masked[:, lower_edge:upper_edge], (((1,), (1,)), ((), ())), preferred_element_type=jnp.float32)
        grad_acc = grad_acc + rounded(partial_value)
    input_grad = grad_acc.astype(jnp.bfloat16)
    product = lax.dot_general(inputs, cotangent, (((0,), (0,)), ((), ())), preferred_element_type=jnp.float32)
    weight_grad = (product * keep_mask * (TOKENS ** -0.5)).astype(jnp.bfloat16)
    return outputs, input_grad, weight_grad
```

```python
import functools

import jax
import jax.numpy as jnp
from jax import lax
from jax.experimental import pallas as pl
from jax.experimental.pallas import tpu as pltpu
from jax.sharding import PartitionSpec as P

BLOCK = 128
PARTS = 2
VMEM_LIMIT = 48 * 1024 * 1024


def tile_of(width):
    return next(t for t in (512, 256, 128) if width % t == 0)


def masked_tile(w_ref, keep_ref, wm_ref):
    for a in range(w_ref.shape[0] // BLOCK):
        rows = slice(a * BLOCK, (a + 1) * BLOCK)
        keep = keep_ref[a : a + 1, :].astype(jnp.bfloat16)
        wm_ref[rows, :] = w_ref[rows, :] * keep


def forward_kernel(n, cols, place_ref, *refs):
    x_refs, (w_ref, keep_ref), (mine_ref, other_ref, whole_ref), (xs, wm) = (
        refs[:cols],
        refs[cols : cols + 2],
        refs[cols + 2 : cols + 5],
        refs[cols + 5 :],
    )
    core, col = place_ref[1], place_ref[2]
    own = x_refs[0].shape[0]
    tr = xs.shape[0] // (2 * n)
    half = n * tr

    @pl.when(pl.program_id(0) == 0)
    def _():
        for k in range(cols):
            at = pl.multiple_of((col ^ k) * own, own)
            whole_ref[pl.ds(at, own), :] = x_refs[k][...]
        for z in range(n):
            for p in range(2):
                at = pl.multiple_of((2 * z + (core ^ p)) * tr, tr)
                xs[pl.ds(p * half + z * tr, tr), :] = whole_ref[pl.ds(at, tr), :]

    masked_tile(w_ref, keep_ref, wm)
    acc = jnp.dot(xs[...], wm[...], preferred_element_type=jnp.float32)
    mine_ref[...] = acc[:half].astype(jnp.bfloat16)
    other_ref[...] = acc[half:].astype(jnp.bfloat16)


def forward(place, xs, weight, keep, part, n):
    depth, width = weight.shape
    tokens = xs[0].shape[0] * len(xs)
    pw = width // PARTS
    t = tile_of(pw)
    steps = pw // t
    const = lambda j, s: (0, 0)
    moving = lambda j, s: (0, part * steps + j)
    out = lambda j, s: (0, j)
    return pl.pallas_call(
        functools.partial(forward_kernel, n, len(xs)),
        grid_spec=pltpu.PrefetchScalarGridSpec(
            num_scalar_prefetch=1,
            grid=(steps,),
            in_specs=[pl.BlockSpec(x.shape, const) for x in xs]
            + [pl.BlockSpec((depth, t), moving), pl.BlockSpec((depth // BLOCK, t), moving)],
            out_specs=[
                pl.BlockSpec((tokens // 2, t), out),
                pl.BlockSpec((tokens // 2, t), out),
                pl.BlockSpec((tokens, depth), const),
            ],
            scratch_shapes=[
                pltpu.VMEM((tokens, depth), jnp.bfloat16),
                pltpu.VMEM((depth, t), jnp.bfloat16),
            ],
        ),
        out_shape=[
            jax.ShapeDtypeStruct((tokens // 2, pw), jnp.bfloat16),
            jax.ShapeDtypeStruct((tokens // 2, pw), jnp.bfloat16),
            jax.ShapeDtypeStruct((tokens, depth), jnp.bfloat16),
        ],
        compiler_params=pltpu.CompilerParams(vmem_limit_bytes=VMEM_LIMIT),
        cost_estimate=pl.CostEstimate(
            flops=2 * tokens * depth * pw, bytes_accessed=2 * pw * (depth + tokens), transcendentals=0
        ),
        name="forward",
    )(place, *xs, weight, keep)


def start_pieces(n, place_ref, pieces, refs, held, sems):
    steps, tokens, t = held.shape
    tr = tokens // (2 * n)
    z, core = place_ref[0], place_ref[1]
    for (kind, s, flip), ref in zip(pieces, refs):
        if kind == "up":
            origin, valid = z - s, z >= s
        elif kind == "down":
            origin, valid = z + s, z + s < n
        else:
            origin = jnp.where(z >= s, z - s, z + s)
            valid = (z >= s) | (z + s < n)

        @pl.when(valid)
        def _():
            at = pl.multiple_of((2 * origin + (core ^ flip)) * tr, tr)

            @pl.loop(0, steps)
            def _(j):
                pltpu.make_async_copy(
                    ref.at[:, pl.ds(pl.multiple_of(j * t, t), t)],
                    held.at[j, pl.ds(at, tr), :],
                    sems.at[j],
                ).start()


def wait_tile(held, sems, j):
    pltpu.make_async_copy(held.at[j], held.at[j], sems.at[j]).wait()


def input_grad_kernel(n, cols, pieces, first, last, place_ref, *refs):
    np_ = len(pieces)
    piece_refs, refs = refs[:np_], refs[np_:]
    (w_ref, keep_ref), refs = refs[:2], refs[2:]
    if not first:
        before_ref, refs = refs[0], refs[1:]
    n_out = cols if last else 1
    out_refs, (held, wm, acc, sems) = refs[:n_out], refs[n_out:]
    j = pl.program_id(0)

    @pl.when(j == 0)
    def _():
        start_pieces(n, place_ref, pieces, piece_refs, held, sems)
        acc[...] = jnp.zeros_like(acc) if first else before_ref[...]

    masked_tile(w_ref, keep_ref, wm)
    wait_tile(held, sems, j)
    acc[...] += lax.dot_general(
        held[j], wm[...], (((1,), (1,)), ((), ())), preferred_element_type=jnp.float32
    )

    @pl.when(j == pl.num_programs(0) - 1)
    def _():
        if last:
            own = out_refs[0].shape[0]
            for k in range(cols):
                at = pl.multiple_of((place_ref[2] ^ k) * own, own)
                out_refs[k][...] = acc[pl.ds(at, own), :].astype(jnp.bfloat16)
        else:
            out_refs[0][...] = acc[...]


def input_grad_part(place, pieces, arrays, weight, keep, before, part, n, cols, tokens):
    depth, width = weight.shape
    pw = width // PARTS
    t = tile_of(pw)
    steps = pw // t
    first, last = before is None, part == PARTS - 1
    const = lambda j, s: (0, 0)
    moving = lambda j, s: (0, part * steps + j)
    if last:
        out_shape = [jax.ShapeDtypeStruct((tokens // cols, depth), jnp.bfloat16)] * cols
    else:
        out_shape = [jax.ShapeDtypeStruct((tokens, depth), jnp.float32)]
    return pl.pallas_call(
        functools.partial(input_grad_kernel, n, cols, pieces, first, last),
        grid_spec=pltpu.PrefetchScalarGridSpec(
            num_scalar_prefetch=1,
            grid=(steps,),
            in_specs=[pl.BlockSpec(memory_space=pl.ANY) for _ in arrays]
            + [pl.BlockSpec((depth, t), moving), pl.BlockSpec((depth // BLOCK, t), moving)]
            + ([] if first else [pl.BlockSpec((tokens, depth), const)]),
            out_specs=[pl.BlockSpec(o.shape, const) for o in out_shape],
            scratch_shapes=[
                pltpu.VMEM((steps, tokens, t), jnp.bfloat16),
                pltpu.VMEM((depth, t), jnp.bfloat16),
                pltpu.VMEM((tokens, depth), jnp.float32),
                pltpu.SemaphoreType.DMA((steps,)),
            ],
        ),
        out_shape=out_shape,
        compiler_params=pltpu.CompilerParams(vmem_limit_bytes=VMEM_LIMIT),
        cost_estimate=pl.CostEstimate(
            flops=2 * tokens * depth * pw, bytes_accessed=2 * pw * (depth + tokens), transcendentals=0
        ),
        name="input_grad",
    )(place, *arrays, weight, keep, *([] if first else [before]))


def weight_grad_kernel(n, pieces, scale, first, place_ref, *refs):
    np_ = len(pieces)
    piece_refs, refs = refs[:np_], refs[np_:]
    (xt_ref, keep_ref), refs = refs[:2], refs[2:]
    if not first:
        refs = refs[1:]
    out_ref, held, sems = refs
    j = pl.program_id(0)

    @pl.when(j == 0)
    def _():
        start_pieces(n, place_ref, pieces, piece_refs, held, sems)

    wait_tile(held, sems, j)
    for a in range(out_ref.shape[0] // BLOCK):
        rows = slice(a * BLOCK, (a + 1) * BLOCK)
        keep = keep_ref[a : a + 1, :] * scale
        acc = jnp.dot(xt_ref[rows, :], held[j], preferred_element_type=jnp.float32)
        out_ref[rows, :] = (acc * keep).astype(jnp.bfloat16)


def weight_grad_part(place, pieces, arrays, xt, keep, before, part, n, width):
    depth, tokens = xt.shape
    pw = width // PARTS
    t = tile_of(pw)
    steps = pw // t
    first = before is None
    const = lambda j, s: (0, 0)
    moving = lambda j, s: (0, part * steps + j)
    return pl.pallas_call(
        functools.partial(weight_grad_kernel, n, pieces, tokens ** (-0.5), first),
        grid_spec=pltpu.PrefetchScalarGridSpec(
            num_scalar_prefetch=1,
            grid=(steps,),
            in_specs=[pl.BlockSpec(memory_space=pl.ANY) for _ in arrays]
            + [pl.BlockSpec((depth, tokens), const), pl.BlockSpec((depth // BLOCK, t), moving)]
            + ([] if first else [pl.BlockSpec(memory_space=pl.ANY)]),
            out_specs=pl.BlockSpec((depth, t), moving),
            scratch_shapes=[
                pltpu.VMEM((steps, tokens, t), jnp.bfloat16),
                pltpu.SemaphoreType.DMA((steps,)),
            ],
        ),
        out_shape=jax.ShapeDtypeStruct((depth, width), jnp.bfloat16),
        input_output_aliases={} if first else {len(arrays) + 3: 0},
        compiler_params=pltpu.CompilerParams(vmem_limit_bytes=VMEM_LIMIT),
        cost_estimate=pl.CostEstimate(
            flops=2 * tokens * depth * pw, bytes_accessed=2 * pw * (depth + tokens), transcendentals=0
        ),
        name="weight_grad",
    )(place, *arrays, xt, keep, *([] if first else [before]))


def local(n, cols, inputs, weight, mask, cotangent):
    row, col = lax.axis_index("row"), lax.axis_index("col")
    z, core = row // 2, row % 2
    place = jnp.stack([z, core, col]).astype(jnp.int32)
    width = weight.shape[1]
    pw = width // PARTS
    tr = cotangent.shape[0]
    tokens = tr * 2 * n

    line = lambda zs, d: [(2 * i + c, 2 * (i + d) + c) for i in zs if 0 <= i + d < n for c in range(2)]
    swap = lambda v: lax.ppermute(v, "row", [(i, i ^ 1) for i in range(2 * n)])
    across = lambda v, k: lax.ppermute(v, "col", [(i, i ^ k) for i in range(cols)])

    cots = [cotangent[:, p * pw : (p + 1) * pw] for p in range(PARTS)]
    xs = [inputs] + [across(inputs, k) for k in range(1, cols)]
    keep = jnp.repeat(mask.astype(jnp.float32), BLOCK, axis=1)

    pieces = [[] for _ in range(PARTS)]
    for p in range(PARTS):
        pieces[p] += [(("up", 0, 0), cots[p]), (("up", 0, 1), swap(cots[p]))]
    ups, downs = list(cots), list(cots)
    for s in range(1, n):
        for p in range(PARTS):
            ups[p] = lax.ppermute(ups[p], "row", line(range(s - 1, n), 1))
            downs[p] = lax.ppermute(downs[p], "row", line(range(0, n - s + 1), -1))
            if 2 * s < n:
                got = [("up", ups[p]), ("down", downs[p])]
            else:
                got = [("either", jnp.where(z >= s, ups[p], downs[p]))]
            for kind, v in got:
                pieces[p] += [((kind, s, 0), v), ((kind, s, 1), swap(v))]

    f32 = jnp.float32
    outs = []
    whole = None
    for p in range(PARTS):
        mine, other, whole_p = forward(place, xs, weight, keep, p, n)
        whole = whole_p if whole is None else whole
        got = swap(other)

        def term(d, mine=mine, got=got):
            at = jnp.clip(d, 0, n - 1) * tr
            cut = lambda v: lax.dynamic_slice_in_dim(v, at, tr, 0).astype(f32)
            return cut(mine) + cut(got)

        up = down = None
        for s in range(1, n):
            u, v = term(z + n - s), term(z - n + s)
            if up is not None:
                u, v = u + up.astype(f32), v + down.astype(f32)
            up = lax.ppermute(u.astype(jnp.bfloat16), "row", line(range(0, s), 1))
            down = lax.ppermute(v.astype(jnp.bfloat16), "row", line(range(n - s, n), -1))
        outs.append((term(z) + up.astype(f32) + down.astype(f32)).astype(jnp.bfloat16))
    outputs = jnp.concatenate(outs, axis=1)

    xt = whole.T
    acc = wg = None
    for p in range(PARTS):
        kinds = [k for k, _ in pieces[p]]
        arrays = [a for _, a in pieces[p]]
        acc = input_grad_part(place, kinds, arrays, weight, keep, acc, p, n, cols, tokens)
        if p < PARTS - 1:
            acc = acc[0]
        wg = weight_grad_part(place, kinds, arrays, xt, keep, wg, p, n, width)
    total = acc[0].astype(f32)
    for k in range(1, cols):
        total = total + across(acc[k], k).astype(f32)
    return outputs, total.astype(jnp.bfloat16), wg


def solution(mesh):
    n, cols = mesh.shape["row"] // 2, mesh.shape["col"]
    return jax.shard_map(
        functools.partial(local, n, cols),
        mesh=mesh,
        in_specs=(P("col", "row"), P("row", "col"), P("row", "col"), P("row", "col")),
        out_specs=(P("row", "col"), P("col", "row"), P("row", "col")),
        check_vma=False,
    )
```

```python
import functools

import jax
import jax.numpy as jnp
from jax import lax
from jax.experimental import pallas as pl
from jax.experimental.pallas import tpu as pltpu
from jax.sharding import PartitionSpec as P

BLOCK = 128
PARTS = 2
AHEAD = 3
COST = 10 ** 11
VMEM_LIMIT = 60 * 1024 * 1024


def tile_of(width):
    return next(t for t in (512, 256, 128) if width % t == 0)


def at_tile(ref, j, t):
    return ref.at[:, pl.ds(j * t, t)]


def token_places(n, cols, tokens, place_ref):
    own, tr = tokens // cols, tokens // (2 * n)
    size = min(own, tr)
    for k in range(cols):
        for i in range(own // size):
            row = (place_ref[2] ^ k) * own + i * size
            r = row // tr
            held = ((r + place_ref[1]) % 2) * (tokens // 2) + (r // 2) * tr + row % tr
            yield k, i * size, pl.multiple_of(held, size), size


def prepare_kernel(w_ref, keep_ref, out_ref, wv, kv, sems, o_sem):
    steps, _, t = out_ref.shape
    loads = [pltpu.make_async_copy(keep_ref, kv, sems.at[0])]
    loads += [pltpu.make_async_copy(w_ref.at[pl.ds(a * BLOCK, BLOCK), :], wv.at[a], sems.at[1 + a]) for a in range(wv.shape[0])]
    for copy in loads[: 1 + AHEAD]:
        copy.start()
    loads[0].wait()
    for a in range(wv.shape[0]):
        loads[1 + a].wait()
        if 1 + a + AHEAD < len(loads):
            loads[1 + a + AHEAD].start()
        for j in range(steps):
            cols = slice(j * t, (j + 1) * t)
            wv[a, :, cols] = wv[a, :, cols] * kv[a : a + 1, cols].astype(wv.dtype)
            pltpu.make_async_copy(wv.at[a, :, pl.ds(j * t, t)], out_ref.at[j, pl.ds(a * BLOCK, BLOCK), :], o_sem).start()
    pltpu.make_async_copy(wv, wv, o_sem).wait()


def prepare(weight, keep):
    depth, width = weight.shape
    t = tile_of(width // PARTS)
    return pl.pallas_call(
        prepare_kernel,
        in_specs=[ANY, ANY],
        out_specs=ANY,
        out_shape=jax.ShapeDtypeStruct((width // t, depth, t), weight.dtype),
        scratch_shapes=[
            pltpu.VMEM((depth // BLOCK, BLOCK, width), weight.dtype),
            pltpu.VMEM((depth // BLOCK, width), jnp.float32),
            pltpu.SemaphoreType.DMA((1 + depth // BLOCK,)),
            pltpu.SemaphoreType.DMA,
        ],
        compiler_params=pltpu.CompilerParams(vmem_limit_bytes=VMEM_LIMIT),
        cost_estimate=pl.CostEstimate(flops=COST, bytes_accessed=COST, transcendentals=0),
        name="prepare",
    )(weight, keep)


def load_weight(w_ref, wv, sems, first):
    return [pltpu.make_async_copy(w_ref.at[first + j], wv.at[j], sems.at[j]) for j in range(wv.shape[0])]


def forward_kernel(n, cols, part, emit, place_ref, *refs):
    x_refs, w_ref = refs[:cols], refs[cols]
    outs, (xs, wv, ov, w_sems, o_sems, x_sem) = refs[cols + 1 : -6], refs[-6:]
    steps, _, t = wv.shape
    tokens = xs.shape[0]
    half = tokens // 2
    for k, at, held, size in token_places(n, cols, tokens, place_ref):
        pltpu.make_async_copy(x_refs[k].at[pl.ds(at, size), :], xs.at[pl.ds(held, size), :], x_sem).start()
    loads = load_weight(w_ref, wv, w_sems, part * steps)
    for copy in loads[:AHEAD]:
        copy.start()
    pltpu.make_async_copy(xs, xs, x_sem).wait()
    stores = []
    if emit:
        stores.append(pltpu.make_async_copy(xs, outs[2], x_sem))
        stores[0].start()
    for j in range(steps):
        loads[j].wait()
        if j + AHEAD < steps:
            loads[j + AHEAD].start()
        acc = jnp.dot(xs[...], wv[j], preferred_element_type=jnp.float32)
        ov[j] = acc.astype(jnp.bfloat16)
        for i in range(2):
            rows = pl.ds(i * half, half)
            stores.append(pltpu.make_async_copy(ov.at[j, rows, :], at_tile(outs[i], j, t), o_sems.at[i, j]))
            stores[-1].start()
    for copy in stores:
        copy.wait()


ANY = pl.BlockSpec(memory_space=pl.ANY)


def call(kernel, name, place, args, out_shape, scratch, aliases=None, after=()):
    held = len(args)
    body = lambda place_ref, *refs: kernel(place_ref, *refs[:held], *refs[held + len(after) :])
    return pl.pallas_call(
        body,
        grid_spec=pltpu.PrefetchScalarGridSpec(
            num_scalar_prefetch=1,
            grid=(),
            in_specs=[ANY] * (held + len(after)),
            out_specs=jax.tree.map(lambda _: ANY, out_shape),
            scratch_shapes=scratch,
        ),
        out_shape=out_shape,
        input_output_aliases=aliases or {},
        compiler_params=pltpu.CompilerParams(vmem_limit_bytes=VMEM_LIMIT),
        cost_estimate=pl.CostEstimate(flops=COST, bytes_accessed=COST, transcendentals=0),
        name=name,
    )(place, *args, *after)


def forward(place, xs, weight, part, n, emit):
    steps, depth, t = weight.shape
    steps //= PARTS
    tokens = xs[0].shape[0] * len(xs)
    bf16 = jnp.bfloat16
    outs = [jax.ShapeDtypeStruct((tokens // 2, steps * t), bf16)] * 2
    return call(
        functools.partial(forward_kernel, n, len(xs), part, emit),
        "forward",
        place,
        [*xs, weight],
        outs + ([jax.ShapeDtypeStruct((tokens, depth), bf16)] if emit else []),
        [
            pltpu.VMEM((tokens, depth), bf16),
            pltpu.VMEM((steps, depth, t), bf16),
            pltpu.VMEM((steps, tokens, t), bf16),
            pltpu.SemaphoreType.DMA((steps,)),
            pltpu.SemaphoreType.DMA((2, steps)),
            pltpu.SemaphoreType.DMA,
        ],
    )


def start_pieces(n, place_ref, pieces, refs, held, sems, first):
    steps, tokens, t = held.shape
    tr = tokens // (2 * n)
    z = place_ref[0]
    for tiles in (range(min(2, steps)), range(min(2, steps), steps)):
        for (link, s, flip, lo, hi), ref in zip(pieces, refs):
            sign = jnp.where(z % 2 == 0, s, -s)
            if link is None:
                origin = z
            elif link == 2:
                origin = jnp.where((z + sign >= 0) & (z + sign < n), z + sign, z - sign)
            else:
                origin = z + sign if link == 0 else z - sign
            mine = [j for j in tiles if lo <= (first + j) * t < hi]

            @pl.when((origin >= 0) & (origin < n))
            def _():
                at = pl.multiple_of(flip * (tokens // 2) + origin * tr, tr)
                for j in mine:
                    source = ref.at[:, pl.ds((first + j) * t - lo, t)]
                    pltpu.make_async_copy(source, held.at[j, pl.ds(at, tr), :], sems.at[j]).start()


def wait_tile(held, sems, j):
    pltpu.make_async_copy(held.at[j], held.at[j], sems.at[j]).wait()


def input_grad_kernel(n, cols, pieces, part, first, last, place_ref, *refs):
    piece_refs, w_ref, refs = refs[: len(pieces)], refs[len(pieces)], refs[len(pieces) + 1 :]
    if not first:
        before_ref, refs = refs[0], refs[1:]
    n_out = cols if last else 1
    out_refs, (held, wv, acc, ob, sems, w_sems, a_sem, o_sem) = refs[:n_out], refs[n_out:]
    steps, tokens, t = held.shape
    loads = load_weight(w_ref, wv, w_sems, part * steps)
    loads[0].start()
    start_pieces(n, place_ref, pieces, piece_refs, held, sems, part * steps)
    for copy in loads[1:AHEAD]:
        copy.start()
    if not first:
        before = pltpu.make_async_copy(before_ref, acc, a_sem)
        before.start()
    for j in range(steps):
        loads[j].wait()
        if j + AHEAD < steps:
            loads[j + AHEAD].start()
        wait_tile(held, sems, j)
        if j == 0 and not first:
            before.wait()
        product = lax.dot_general(held[j], wv[j], (((1,), (1,)), ((), ())), preferred_element_type=jnp.float32)
        if j == 0 and first:
            acc[...] = product
        else:
            acc[...] += product
    if last:
        ob[...] = acc[...].astype(jnp.bfloat16)
        for k, at, row, size in token_places(n, cols, tokens, place_ref):
            pltpu.make_async_copy(ob.at[pl.ds(row, size), :], out_refs[k].at[pl.ds(at, size), :], o_sem).start()
        pltpu.make_async_copy(ob, ob, o_sem).wait()
    else:
        store = pltpu.make_async_copy(acc, out_refs[0], o_sem)
        store.start()
        store.wait()


def input_grad_part(place, pieces, arrays, weight, before, after, part, n, cols, tokens):
    steps, depth, t = weight.shape
    steps //= PARTS
    first, last = before is None, part == PARTS - 1
    f32, bf16 = jnp.float32, jnp.bfloat16
    if last:
        out_shape = [jax.ShapeDtypeStruct((tokens // cols, depth), bf16)] * cols
    else:
        out_shape = [jax.ShapeDtypeStruct((tokens, depth), f32)]
    return call(
        functools.partial(input_grad_kernel, n, cols, pieces, part, first, last),
        "input_grad",
        place,
        [*arrays, weight] + ([] if first else [before]),
        out_shape,
        [
            pltpu.VMEM((steps, tokens, t), bf16),
            pltpu.VMEM((steps, depth, t), bf16),
            pltpu.VMEM((tokens, depth), f32),
            pltpu.VMEM((tokens, depth), bf16),
            pltpu.SemaphoreType.DMA((steps,)),
            pltpu.SemaphoreType.DMA((steps,)),
            pltpu.SemaphoreType.DMA,
            pltpu.SemaphoreType.DMA,
        ],
        after=after,
    )


def weight_grad_kernel(n, pieces, part, scale, first, place_ref, *refs):
    piece_refs, (xt_ref, keep_ref), refs = refs[: len(pieces)], refs[len(pieces) : len(pieces) + 2], refs[len(pieces) + 2 :]
    out_ref, held, xt, kv, ov, sems, x_sems, o_sems = refs[0 if first else 1 :]
    steps, _, t = held.shape
    loads = [
        pltpu.make_async_copy(xt_ref, xt, x_sems.at[0]),
        pltpu.make_async_copy(keep_ref.at[:, pl.ds(part * steps * t, steps * t)], kv, x_sems.at[1]),
    ]
    for copy in loads:
        copy.start()
    start_pieces(n, place_ref, pieces, piece_refs, held, sems, part * steps)
    for copy in loads:
        copy.wait()
    stores = []
    for j in range(steps):
        wait_tile(held, sems, j)
        acc = jnp.dot(xt[...], held[j], preferred_element_type=jnp.float32)
        for a in range(xt.shape[0] // BLOCK):
            rows = slice(a * BLOCK, (a + 1) * BLOCK)
            keep = kv[a : a + 1, j * t : (j + 1) * t] * scale
            ov[j, rows, :] = (acc[rows, :] * keep).astype(jnp.bfloat16)
        stores.append(pltpu.make_async_copy(ov.at[j], at_tile(out_ref, part * steps + j, t), o_sems.at[j]))
        stores[-1].start()
    for copy in stores:
        copy.wait()


def weight_grad_part(place, pieces, arrays, xt, keep, before, after, part, n, width):
    depth, tokens = xt.shape
    t = tile_of(width // PARTS)
    steps = width // PARTS // t
    first = before is None
    bf16 = jnp.bfloat16
    return call(
        functools.partial(weight_grad_kernel, n, pieces, part, tokens ** (-0.5), first),
        "weight_grad",
        place,
        [*arrays, xt, keep] + ([] if first else [before]),
        jax.ShapeDtypeStruct((depth, width), bf16),
        [
            pltpu.VMEM((steps, tokens, t), bf16),
            pltpu.VMEM((depth, tokens), bf16),
            pltpu.VMEM((depth // BLOCK, steps * t), jnp.float32),
            pltpu.VMEM((steps, depth, t), bf16),
            pltpu.SemaphoreType.DMA((steps,)),
            pltpu.SemaphoreType.DMA((2,)),
            pltpu.SemaphoreType.DMA((steps,)),
        ],
        {} if first else {len(arrays) + 3: 0},
        after,
    )


def local(n, cols, inputs, weight, mask, cotangent):
    row, col = lax.axis_index("row"), lax.axis_index("col")
    z, core = row // 2, row % 2
    place = jnp.stack([z, core, col]).astype(jnp.int32)
    width = weight.shape[1]
    pw = width // PARTS
    tr = cotangent.shape[0]
    tokens = tr * 2 * n

    even = z % 2 == 0
    up = [(2 * i + c, 2 * (i + 1) + c) for i in range(n - 1) for c in range(2)]
    links = [[e for i, j in up if (i // 2) % 2 == odd for e in ((i, j), (j, i))] for odd in range(2)]
    for pairs in links:
        pairs += [(i, i ^ 1) for i in sorted(set(range(2 * n)) - {i for i, _ in pairs})]
    other_side = jnp.where(even, z - 1, z + 1)
    has = [jnp.where(even, z + 1, z - 1) < n, (other_side >= 0) & (other_side < n)]
    exchange = lambda v, link: lax.ppermute(v, "row", links[link])
    swap = lambda v: lax.ppermute(v, "row", [(i, i ^ 1) for i in range(2 * n)])
    across = lambda v, k: lax.ppermute(v, "col", [(i, i ^ k) for i in range(cols)])

    f32, bf16 = jnp.float32, jnp.bfloat16
    xs = [inputs] + [across(inputs, k) for k in range(1, cols)]
    got = [exchange(cotangent, link) for link in range(2)]
    keep = jnp.repeat(mask.astype(f32), BLOCK, axis=1)
    pieces = [((None, 0, 0, 0, width), cotangent), ((None, 0, 1, 0, width), swap(cotangent))]

    def keep_pieces(s, lo, pair):
        hi = lo + pair[0].shape[1]
        if 2 * s < n:
            held = list(enumerate(pair))
        else:
            origin = jnp.where(even, z + s, z - s)
            first = (origin >= 0) & (origin < n)
            held = [(2, jnp.where(first, *pair))]
        for link, v in held:
            pieces.extend([((link, s, 0, lo, hi), v), ((link, s, 1, lo, hi), swap(v))])

    keep_pieces(1, 0, got)
    first, got = got, [[v[:, p * pw : (p + 1) * pw] for v in got] for p in range(PARTS)]

    masked = prepare(weight, keep)
    mine, theirs = [], []
    for p in range(PARTS):
        m, other, *more = forward(place, xs, masked, p, n, p == 0)
        whole = more[0] if more else whole
        mine.append(m)
        theirs.append(swap(other))

    def term(p, d):
        at = jnp.clip(d, 0, n - 1) * tr
        cut = lambda v: lax.dynamic_slice_in_dim(v, at, tr, 0).astype(f32)
        return cut(mine[p]) + cut(theirs[p])

    sent = [None] * PARTS
    for k in range(2, n + 1):
        for p in range(PARTS):
            if k > 2:
                keep_pieces(k - 1, p * pw, got[p])
            send = []
            if k == 2 and p:
                got[p] = [v[:, p * pw : (p + 1) * pw] for v in lax.optimization_barrier((*first, *got[p - 1]))[:2]]
            for link in range(2):
                upward = even if link == 0 else ~even
                d = jnp.where(upward, z + n - k + 1, z - n + k - 1)
                own = jnp.where((d >= 0) & (d < n), term(p, d), 0.0)
                came = jnp.where(has[1 - link], got[p][1 - link].astype(f32), 0.0)
                send.append((came + own).astype(bf16))
            got[p] = [exchange(v, link) for link, v in enumerate(send)]
            sent[p] = send
    outputs = jnp.zeros((tr, width), bf16)
    for p in range(PARTS):
        total = term(p, z)
        for link in range(2):
            total += jnp.where(has[link], got[p][link].astype(f32), 0.0)
        outputs = lax.dynamic_update_slice(outputs, total.astype(bf16), (0, p * pw))

    xt = whole.T
    acc = wg = None
    for p in range(PARTS):
        own = [(k, v) for k, v in pieces if k[3] < (p + 1) * pw and k[4] > p * pw]
        kinds, arrays = [k for k, _ in own], [v for _, v in own]
        last = p == PARTS - 1
        acc = input_grad_part(place, kinds, arrays, masked, acc, sent[p] if p == 0 else [wg], p, n, cols, tokens)
        if not last:
            acc = acc[0]
        wg = weight_grad_part(place, kinds, arrays, xt, keep, wg, [outputs] if last else sent[p + 1], p, n, width)
    total = acc[0].astype(f32)
    for k in range(1, cols):
        total = total + across(acc[k], k).astype(f32)
    return outputs, total.astype(bf16), wg


def solution(mesh):
    n, cols = mesh.shape["row"] // 2, mesh.shape["col"]
    return jax.shard_map(
        functools.partial(local, n, cols),
        mesh=mesh,
        in_specs=(P("col", "row"), P("row", "col"), P("row", "col"), P("row", "col")),
        out_specs=(P("row", "col"), P("col", "row"), P("row", "col")),
        check_vma=False,
    )
```

```python
import functools

import jax
import jax.numpy as jnp
from jax import lax
from jax.experimental import pallas as pl
from jax.experimental.pallas import tpu as pltpu
from jax.sharding import PartitionSpec as P

BLOCK = 128
PARTS = 2
AHEAD = 2
ROWS_AHEAD = 4
COST = 10 ** 11
VMEM_LIMIT = 60 * 1024 * 1024


def tile_of(width):
    return next(t for t in (512, 256, 128) if width % t == 0)


def at_tile(ref, j, t):
    return ref.at[:, pl.ds(j * t, t)]


def token_places(n, cols, tokens, place_ref):
    own, tr = tokens // cols, tokens // (2 * n)
    size = min(own, tr)
    for k in range(cols):
        for i in range(own // size):
            row = (place_ref[2] ^ k) * own + i * size
            r = row // tr
            held = ((r + place_ref[1]) % 2) * (tokens // 2) + (r // 2) * tr + row % tr
            yield k, i * size, pl.multiple_of(held, size), size


def mask_tile(tile_ref, keep):
    for a in range(tile_ref.shape[0] // BLOCK):
        rows = slice(a * BLOCK, (a + 1) * BLOCK)
        tile_ref[rows, :] = tile_ref[rows, :] * keep[a : a + 1, :].astype(tile_ref.dtype)


def load_weight(w_ref, keep_ref, wv, kv, sems, part):
    steps, _, t = wv.shape
    copies = [pltpu.make_async_copy(keep_ref.at[:, pl.ds(part * steps * t, steps * t)], kv, sems.at[steps])]
    return copies + [pltpu.make_async_copy(at_tile(w_ref, part * steps + j, t), wv.at[j], sems.at[j]) for j in range(steps)]


def forward_kernel(n, cols, part, emit, place_ref, *refs):
    x_refs, (w_ref, keep_ref) = refs[:cols], refs[cols : cols + 2]
    outs, (xs, wv, kv, ov, w_sems, o_sems, x_sem) = refs[cols + 2 : -7], refs[-7:]
    steps, _, t = wv.shape
    tokens = xs.shape[0]
    half = tokens // 2
    for k, at, held, size in token_places(n, cols, tokens, place_ref):
        pltpu.make_async_copy(x_refs[k].at[pl.ds(at, size), :], xs.at[pl.ds(held, size), :], x_sem).start()
    loads = load_weight(w_ref, keep_ref, wv, kv, w_sems, part)
    for copy in loads[: 1 + AHEAD]:
        copy.start()
    pltpu.make_async_copy(xs, xs, x_sem).wait()
    stores = []
    if emit:
        stores.append(pltpu.make_async_copy(xs, outs[2], x_sem))
        stores[0].start()
    loads[0].wait()
    for j in range(steps):
        loads[1 + j].wait()
        if j + AHEAD < steps:
            loads[1 + j + AHEAD].start()
        mask_tile(wv.at[j], kv[:, j * t : (j + 1) * t])
        acc = jnp.dot(xs[...], wv[j], preferred_element_type=jnp.float32)
        ov[j] = acc.astype(jnp.bfloat16)
        for i in range(2):
            rows = pl.ds(i * half, half)
            stores.append(pltpu.make_async_copy(ov.at[j, rows, :], at_tile(outs[i], j, t), o_sems.at[i, j]))
            stores[-1].start()
    for copy in stores:
        copy.wait()


ANY = pl.BlockSpec(memory_space=pl.ANY)


def call(kernel, name, place, args, out_shape, scratch, aliases=None, after=(), cost=COST):
    held = len(args)
    body = lambda place_ref, *refs: kernel(place_ref, *refs[:held], *refs[held + len(after) :])
    return pl.pallas_call(
        body,
        grid_spec=pltpu.PrefetchScalarGridSpec(
            num_scalar_prefetch=1,
            grid=(),
            in_specs=[ANY] * (held + len(after)),
            out_specs=jax.tree.map(lambda _: ANY, out_shape),
            scratch_shapes=scratch,
        ),
        out_shape=out_shape,
        input_output_aliases=aliases or {},
        compiler_params=pltpu.CompilerParams(vmem_limit_bytes=VMEM_LIMIT),
        cost_estimate=pl.CostEstimate(flops=cost, bytes_accessed=cost, transcendentals=0),
        name=name,
    )(place, *args, *after)


def pause_kernel(place_ref, out_ref, held, sem):
    held[...] = jnp.zeros_like(held)
    store = pltpu.make_async_copy(held, out_ref, sem)
    store.start()
    store.wait()


def pause(place, after):
    shape = (8, 128)
    return call(
        pause_kernel,
        "pause",
        place,
        [],
        jax.ShapeDtypeStruct(shape, jnp.float32),
        [pltpu.VMEM(shape, jnp.float32), pltpu.SemaphoreType.DMA],
        after=after,
    )


def forward(place, xs, weight, keep, after, part, n, emit):
    depth, width = weight.shape
    t = tile_of(width // PARTS)
    steps = width // PARTS // t
    tokens = xs[0].shape[0] * len(xs)
    bf16 = jnp.bfloat16
    outs = [jax.ShapeDtypeStruct((tokens // 2, steps * t), bf16)] * 2
    return call(
        functools.partial(forward_kernel, n, len(xs), part, emit),
        "forward",
        place,
        [*xs, weight, keep],
        outs + ([jax.ShapeDtypeStruct((tokens, depth), bf16)] if emit else []),
        [
            pltpu.VMEM((tokens, depth), bf16),
            pltpu.VMEM((steps, depth, t), bf16),
            pltpu.VMEM((depth // BLOCK, steps * t), jnp.float32),
            pltpu.VMEM((steps, tokens, t), bf16),
            pltpu.SemaphoreType.DMA((steps + 1,)),
            pltpu.SemaphoreType.DMA((2, steps)),
            pltpu.SemaphoreType.DMA,
        ],
        after=after,
    )


def origin_of(n, z, piece):
    link, s, _ = piece
    sign = jnp.where(z % 2 == 0, s, -s)
    if link == 2:
        return jnp.where((z + sign >= 0) & (z + sign < n), z + sign, z - sign)
    return z - sign if link == 1 else z + sign


def groups_of(steps):
    ends = sorted({min(e, steps) for e in (1, 4, steps)})
    return list(zip([0, *ends], ends))


def start_pieces(n, place_ref, pieces, refs, held, sems, t):
    tokens, width = held.shape
    tr = tokens // (2 * n)
    for g, (lo, hi) in enumerate(groups_of(width // t)):
        for piece, ref in zip(pieces, refs):
            origin = origin_of(n, place_ref[0], piece)

            @pl.when((origin >= 0) & (origin < n))
            def _():
                at = pl.multiple_of(piece[2] * (tokens // 2) + origin * tr, tr)
                columns = pl.ds(lo * t, (hi - lo) * t)
                pltpu.make_async_copy(ref.at[:, columns], held.at[pl.ds(at, tr), columns], sems.at[g]).start()


def each_piece(n, place_ref, pieces, body):
    for i, piece in enumerate(pieces):
        origin = origin_of(n, place_ref[0], piece)
        pl.when((origin >= 0) & (origin < n))(functools.partial(body, i, origin))


def product_rows(n, place_ref, pieces, piece_refs, w_ref, keep_ref, held, wv, kv, acc, sems, w_sems):
    steps, _, t = wv.shape
    tr = held.shape[0] // len(pieces)
    loads = load_weight(w_ref, keep_ref, wv, kv, w_sems, 0)
    for copy in loads[:2]:
        copy.start()

    def rows_of(i):
        return pltpu.make_async_copy(piece_refs[i], held.at[pl.ds(i * tr, tr), :], sems.at[i])

    each_piece(n, place_ref, pieces, lambda i, _: rows_of(i).start())
    for copy in loads[2 : 1 + ROWS_AHEAD]:
        copy.start()
    each_piece(n, place_ref, pieces, lambda i, _: rows_of(i).wait())
    loads[0].wait()
    for j in range(steps):
        loads[1 + j].wait()
        if j + ROWS_AHEAD < steps:
            loads[1 + j + ROWS_AHEAD].start()
        columns = slice(j * t, (j + 1) * t)
        mask_tile(wv.at[j], kv[:, columns])
        product = lax.dot_general(held[:, columns], wv[j], (((1,), (1,)), ((), ())), preferred_element_type=jnp.float32)
        if j == 0:
            acc[...] = product
        else:
            acc[...] += product


def early_kernel(n, pieces, place_ref, *refs):
    piece_refs, (w_ref, keep_ref, out_ref, held, wv, kv, acc, ob, sems, w_sems, o_sem) = refs[: len(pieces)], refs[len(pieces) :]
    product_rows(n, place_ref, pieces, piece_refs, w_ref, keep_ref, held, wv, kv, acc, sems, w_sems)
    ob[...] = acc[...].astype(jnp.bfloat16)
    store = pltpu.make_async_copy(ob, out_ref, o_sem)
    store.start()
    store.wait()


def early_rows(place, n, pieces, arrays, weight, keep, after):
    depth, width = weight.shape
    t = tile_of(width // PARTS)
    steps = width // t
    rows = len(pieces) * arrays[0].shape[0]
    f32, bf16 = jnp.float32, jnp.bfloat16
    return call(
        functools.partial(early_kernel, n, pieces),
        "early_rows",
        place,
        [*arrays, weight, keep],
        jax.ShapeDtypeStruct((rows, depth), bf16),
        [
            pltpu.VMEM((rows, width), bf16),
            pltpu.VMEM((steps, depth, t), bf16),
            pltpu.VMEM((depth // BLOCK, width), f32),
            pltpu.VMEM((rows, depth), f32),
            pltpu.VMEM((rows, depth), bf16),
            pltpu.SemaphoreType.DMA((len(pieces),)),
            pltpu.SemaphoreType.DMA((steps + 1,)),
            pltpu.SemaphoreType.DMA,
        ],
        after=after,
    )


def late_kernel(n, cols, early, late, place_ref, *refs):
    piece_refs, (w_ref, keep_ref, early_ref), refs = refs[: len(late)], refs[len(late) : len(late) + 3], refs[len(late) + 3 :]
    out_refs, (held, wv, kv, acc, ob, sems, w_sems, e_sems, o_sem) = refs[:cols], refs[cols:]
    tokens = ob.shape[0]
    tr = tokens // (2 * n)
    rows = lambda piece, origin: pl.ds(pl.multiple_of(piece[2] * (tokens // 2) + origin * tr, tr), tr)

    def early_of(i, origin):
        return pltpu.make_async_copy(early_ref.at[pl.ds(i * tr, tr), :], ob.at[rows(early[i], origin), :], e_sems.at[i])

    each_piece(n, place_ref, early, lambda i, origin: early_of(i, origin).start())
    product_rows(n, place_ref, late, piece_refs, w_ref, keep_ref, held, wv, kv, acc, sems, w_sems)
    each_piece(n, place_ref, early, lambda i, origin: early_of(i, origin).wait())

    def store(i, origin):
        ob[rows(late[i], origin), :] = acc[i * tr : (i + 1) * tr, :].astype(jnp.bfloat16)

    each_piece(n, place_ref, late, store)
    for k, at, row, size in token_places(n, cols, tokens, place_ref):
        pltpu.make_async_copy(ob.at[pl.ds(row, size), :], out_refs[k].at[pl.ds(at, size), :], o_sem).start()
    pltpu.make_async_copy(ob, ob, o_sem).wait()


def late_rows(place, early, late, arrays, weight, keep, done, after, n, cols):
    depth, width = weight.shape
    tr = arrays[0].shape[0]
    tokens = 2 * n * tr
    t = tile_of(width // PARTS)
    steps = width // t
    f32, bf16 = jnp.float32, jnp.bfloat16
    rows = len(late) * tr
    return call(
        functools.partial(late_kernel, n, cols, early, late),
        "late_rows",
        place,
        [*arrays, weight, keep, done],
        [jax.ShapeDtypeStruct((tokens // cols, depth), bf16)] * cols,
        [
            pltpu.VMEM((rows, width), bf16),
            pltpu.VMEM((steps, depth, t), bf16),
            pltpu.VMEM((depth // BLOCK, width), f32),
            pltpu.VMEM((rows, depth), f32),
            pltpu.VMEM((tokens, depth), bf16),
            pltpu.SemaphoreType.DMA((len(late),)),
            pltpu.SemaphoreType.DMA((steps + 1,)),
            pltpu.SemaphoreType.DMA((len(early),)),
            pltpu.SemaphoreType.DMA,
        ],
        after=after,
    )


def send_kernel(n, k, links, behind, place_ref, *refs):
    mine_ref, theirs_ref, refs = refs[0], refs[1], refs[2:]
    came_refs, refs = refs[: len(behind)], refs[len(behind) :]
    out_refs, (terms, cv, ov, sems, o_sems) = refs[: len(links)], refs[len(links) :]
    tr = ov.shape[1]
    z = place_ref[0]
    odd = lax.rem(z, 2)

    def each_link(body):
        for i, link in enumerate(links):
            upward = odd == link
            d = jnp.where(upward, z + n - k + 1, z - n + k - 1)
            pl.when((d >= 0) & (d < n))(functools.partial(body, i, link, d))

    def load(i, link, d):
        for h, ref in enumerate((mine_ref, theirs_ref)):
            source = ref.at[pl.ds(pl.multiple_of(d * tr, tr), tr), :]
            pltpu.make_async_copy(source, terms.at[i, h], sems.at[i]).start()
        if 1 - link in behind:
            pltpu.make_async_copy(came_refs[behind.index(1 - link)], cv.at[i], sems.at[len(links) + i]).start()

    def add(i, link, d):
        pltpu.make_async_copy(terms.at[i], terms.at[i], sems.at[i]).wait()
        total = terms[i, 0].astype(jnp.float32) + terms[i, 1].astype(jnp.float32)
        if 1 - link in behind:
            pltpu.make_async_copy(cv.at[i], cv.at[i], sems.at[len(links) + i]).wait()
            other = z + 1 - 2 * odd if link == 1 else z - 1 + 2 * odd
            total += jnp.where((other >= 0) & (other < n), cv[i].astype(jnp.float32), 0.0)
        ov[i] = total.astype(jnp.bfloat16)
        pltpu.make_async_copy(ov.at[i], out_refs[i], o_sems.at[i]).start()

    each_link(load)
    each_link(add)
    each_link(lambda i, link, d: pltpu.make_async_copy(ov.at[i], out_refs[i], o_sems.at[i]).wait())


def send_sums(place, mine, theirs, came, links, after, k, n):
    behind = tuple(link for link in range(2) if came[link] is not None)
    pw = mine.shape[1]
    tr = mine.shape[0] // n
    bf16 = jnp.bfloat16
    return call(
        functools.partial(send_kernel, n, k, links, behind),
        "send_sums",
        place,
        [mine, theirs, *(came[link] for link in behind)],
        [jax.ShapeDtypeStruct((tr, pw), bf16)] * len(links),
        [
            pltpu.VMEM((len(links), 2, tr, pw), bf16),
            pltpu.VMEM((len(links), tr, pw), bf16),
            pltpu.VMEM((len(links), tr, pw), bf16),
            pltpu.SemaphoreType.DMA((2 * len(links),)),
            pltpu.SemaphoreType.DMA((len(links),)),
        ],
        after=after,
        cost=1 if k < n else COST,
    )


def weight_grad_kernel(n, pieces, scale, place_ref, *refs):
    piece_refs, (xt_ref, keep_ref, out_ref, held, xt, kv, ov, sems, x_sems, o_sems) = refs[: len(pieces)], refs[len(pieces) :]
    steps, _, t = ov.shape
    loads = [pltpu.make_async_copy(xt_ref, xt, x_sems.at[0]), pltpu.make_async_copy(keep_ref, kv, x_sems.at[1])]
    for copy in loads:
        copy.start()
    start_pieces(n, place_ref, pieces, piece_refs, held, sems, t)
    groups = groups_of(steps)
    for copy in loads:
        copy.wait()
    stores = []
    for j in range(steps):
        for g, (lo, hi) in enumerate(groups):
            if lo == j:
                part = held.at[:, pl.ds(lo * t, (hi - lo) * t)]
                pltpu.make_async_copy(part, part, sems.at[g]).wait()
        acc = jnp.dot(xt[...], held[:, j * t : (j + 1) * t], preferred_element_type=jnp.float32)
        for a in range(xt.shape[0] // BLOCK):
            rows = slice(a * BLOCK, (a + 1) * BLOCK)
            keep = kv[a : a + 1, j * t : (j + 1) * t] * scale
            ov[j, rows, :] = (acc[rows, :] * keep).astype(jnp.bfloat16)
        stores.append(pltpu.make_async_copy(ov.at[j], at_tile(out_ref, j, t), o_sems.at[j]))
        stores[-1].start()
    for copy in stores:
        copy.wait()


def weight_grad(place, pieces, arrays, xt, keep, n, width):
    depth, tokens = xt.shape
    t = tile_of(width // PARTS)
    steps = width // t
    bf16 = jnp.bfloat16
    return call(
        functools.partial(weight_grad_kernel, n, pieces, tokens ** (-0.5)),
        "weight_grad",
        place,
        [*arrays, xt, keep],
        jax.ShapeDtypeStruct((depth, width), bf16),
        [
            pltpu.VMEM((tokens, width), bf16),
            pltpu.VMEM((depth, tokens), bf16),
            pltpu.VMEM((depth // BLOCK, width), jnp.float32),
            pltpu.VMEM((steps, depth, t), bf16),
            pltpu.SemaphoreType.DMA((len(groups_of(steps)),)),
            pltpu.SemaphoreType.DMA((2,)),
            pltpu.SemaphoreType.DMA((steps,)),
        ],
    )


def finish_kernel(n, cols, links, place_ref, *refs):
    z = place_ref[0]
    each = 2 + len(links)
    sum_refs, grad_refs, (out_ref, grad_ref, sv, gv, ov, ob, sems, o_sems) = (
        refs[: each * PARTS],
        refs[each * PARTS : each * PARTS + cols],
        refs[each * PARTS + cols :],
    )
    tr, pw = sv.shape[-2:]
    for p in range(PARTS):
        for i in range(each):
            ref = sum_refs[each * p + i]
            if i < 2:
                ref = ref.at[pl.ds(pl.multiple_of(z * tr, tr), tr), :]
            pltpu.make_async_copy(ref, sv.at[p, i], sems.at[p]).start()
    for k in range(cols):
        pltpu.make_async_copy(grad_refs[k], gv.at[k], sems.at[PARTS]).start()
    odd = lax.rem(z, 2)
    stores = []
    for p in range(PARTS):
        pltpu.make_async_copy(sv.at[p], sv.at[p], sems.at[p]).wait()
        total = sv[p, 0].astype(jnp.float32) + sv[p, 1].astype(jnp.float32)
        for i, link in enumerate(links):
            other = z + 1 - 2 * odd if link == 0 else z - 1 + 2 * odd
            came = sv[p, 2 + i].astype(jnp.float32)
            total += jnp.where((other >= 0) & (other < n), came, 0.0)
        ov[p] = total.astype(jnp.bfloat16)
        stores.append(pltpu.make_async_copy(ov.at[p], out_ref.at[:, pl.ds(p * pw, pw)], o_sems.at[p]))
        stores[-1].start()
    pltpu.make_async_copy(gv, gv, sems.at[PARTS]).wait()
    total = gv[0].astype(jnp.float32)
    for k in range(1, cols):
        total += gv[k].astype(jnp.float32)
    ob[...] = total.astype(jnp.bfloat16)
    stores.append(pltpu.make_async_copy(ob, grad_ref, o_sems.at[PARTS]))
    stores[-1].start()
    for copy in stores:
        copy.wait()


def finish(place, sums, grads, links, n):
    tr, pw = sums[0][-1].shape
    rows, depth = grads[0].shape
    cols = len(grads)
    bf16 = jnp.bfloat16
    return call(
        functools.partial(finish_kernel, n, cols, links),
        "finish",
        place,
        [v for part in sums for v in part] + grads,
        [jax.ShapeDtypeStruct((tr, pw * PARTS), bf16), jax.ShapeDtypeStruct((rows, depth), bf16)],
        [
            pltpu.VMEM((PARTS, 2 + len(links), tr, pw), bf16),
            pltpu.VMEM((cols, rows, depth), bf16),
            pltpu.VMEM((PARTS, tr, pw), bf16),
            pltpu.VMEM((rows, depth), bf16),
            pltpu.SemaphoreType.DMA((PARTS + 1,)),
            pltpu.SemaphoreType.DMA((PARTS + 1,)),
        ],
    )


def local(n, cols, inputs, weight, mask, cotangent):
    row, col = lax.axis_index("row"), lax.axis_index("col")
    z, core = row // 2, row % 2
    place = jnp.stack([z, core, col]).astype(jnp.int32)
    width = weight.shape[1]
    pw = width // PARTS
    tr = cotangent.shape[0]
    tokens = tr * 2 * n

    f32, bf16 = jnp.float32, jnp.bfloat16
    swap = lambda v: lax.ppermute(v, "row", [(i, i ^ 1) for i in range(2 * n)])
    across = lambda v, k: lax.ppermute(v, "col", [(i, i ^ k) for i in range(cols)])

    def pairs_of(link, ups, downs):
        pairs = [(i, i + 1) for i in ups if i % 2 == link and i + 1 < n]
        return pairs + [(i, i - 1) for i in downs if i % 2 != link and i > 0]

    def over(v, link, ups, downs):
        pairs = pairs_of(link, ups, downs)
        if not pairs:
            return None
        pairs = [(2 * i + c, 2 * j + c) for i, j in pairs for c in range(2)]
        if {i for i, _ in pairs} == {j for _, j in pairs}:
            pairs += [(i, i ^ 1) for i in sorted(set(range(2 * n)) - {i for i, _ in pairs})]
        return lax.ppermute(v, "row", pairs)

    even = z % 2 == 0

    xs = [inputs] + [across(inputs, k) for k in range(1, cols)]
    keep = jnp.repeat(mask.astype(f32), BLOCK, axis=1)
    came = [over(cotangent, link, range(n), range(n)) for link in range(2)]
    first = came
    pieces = [((0, 0, 0), cotangent), ((0, 0, 1), swap(cotangent))]

    def keep_pieces(s):
        have = [(link, v) for link, v in enumerate(came) if v is not None]
        if len(have) == 2 and 2 * s >= n:
            origin = jnp.where(even, z + s, z - s)
            have = [(2, jnp.where((origin >= 0) & (origin < n), *came))]
        for link, v in have:
            pieces.extend([((link, s, 0), v), ((link, s, 1), swap(v))])

    keep_pieces(1)

    mine, theirs = [], []
    for p in range(PARTS):
        m, other, *more = forward(place, xs, weight, keep, first if p else (), p, n, p == 0)
        whole = more[0] if more else whole
        mine.append(m)
        theirs.append(swap(other))
    xt = whole.T

    sums = [[None, None] for _ in range(PARTS)]
    sent = {}

    def slot(k, p, after):
        ups, downs = range(k - 1), range(n - k + 1, n)
        links = tuple(link for link in range(2) if pairs_of(link, ups, downs))
        sent[k, p] = send_sums(place, mine[p], theirs[p], sums[p], links, after, k, n)
        sums[p] = [None, None]
        for link, v in zip(links, sent[k, p]):
            sums[p][link] = over(v, link, ups, downs)

    after = ()
    for k in range(2, n + 1):
        if k < n:
            came = [
                None if came[1 - link] is None else over(came[1 - link], link, range(k - 1, n), range(n - k + 1))
                for link in range(2)
            ]
        slot(k, 0, after)
        after = sent[k, 0]
        if k == 2:
            came, after = lax.optimization_barrier((came, after))
            after = [*after, *(v for v in came if v is not None)]
        if k == n:
            late = [(i, v) for i, v in pieces if 2 * i[1] >= n]
            parts = late_rows(
                place, kinds, [i for i, _ in late], [v for _, v in late], weight, keep, early, after, n, cols
            )
            after = parts
        for p in range(1, PARTS):
            slot(k, p, after)
            after = sent[k, p]
        if k == 2:
            held = [(i, v) for i, v in pieces if 2 * i[1] < n]
            kinds = [i for i, _ in held]
            early = early_rows(place, n, kinds, [v for _, v in held], weight, keep, after)
            after = [early]
        elif k < n:
            after = [pause(place, after)]
            came, after = lax.optimization_barrier((came, after))
        if k < n:
            keep_pieces(k)
    grads = [parts[0]] + [across(parts[k], k) for k in range(1, cols)]
    wg = weight_grad(place, [k for k, _ in pieces], [v for _, v in pieces], xt, keep, n, width)
    links = [link for link in range(2) if sums[0][link] is not None]
    ends = [[mine[p], theirs[p], *(sums[p][link] for link in links)] for p in range(PARTS)]
    outputs, input_grad = finish(place, ends, grads, links, n)
    return outputs, input_grad, wg


def solution(mesh):
    n, cols = mesh.shape["row"] // 2, mesh.shape["col"]
    return jax.shard_map(
        functools.partial(local, n, cols),
        mesh=mesh,
        in_specs=(P("col", "row"), P("row", "col"), P("row", "col"), P("row", "col")),
        out_specs=(P("row", "col"), P("col", "row"), P("row", "col")),
        check_vma=False,
    )
```

```python
import functools

import jax
import jax.numpy as jnp
from jax import lax
from jax.experimental import pallas as pl
from jax.experimental.pallas import tpu as pltpu
from jax.sharding import PartitionSpec as P

BLOCK = 128
PARTS = 2
AHEAD = 2
ROWS_AHEAD = 4
COST = 10 ** 11
VMEM_LIMIT = 64 * 1024 * 1024


def tile_of(width):
    return next(t for t in (512, 256, 128) if width % t == 0)


def at_tile(ref, j, t):
    return ref.at[:, pl.ds(j * t, t)]


def token_places(n, cols, tokens, place_ref):
    own, tr = tokens // cols, tokens // (2 * n)
    size = min(own, tr)
    for k in range(cols):
        for i in range(own // size):
            row = (place_ref[2] ^ k) * own + i * size
            r = row // tr
            held = ((r + place_ref[1]) % 2) * (tokens // 2) + (r // 2) * tr + row % tr
            yield k, i * size, pl.multiple_of(held, size), size


def mask_tile(tile_ref, keep):
    for a in range(tile_ref.shape[0] // BLOCK):
        rows = slice(a * BLOCK, (a + 1) * BLOCK)
        tile_ref[rows, :] = tile_ref[rows, :] * keep[a : a + 1, :].astype(tile_ref.dtype)


def load_weight(w_ref, keep_ref, wv, kv, sems, part):
    steps, _, t = wv.shape
    copies = [pltpu.make_async_copy(keep_ref.at[:, pl.ds(part * steps * t, steps * t)], kv, sems.at[steps])]
    return copies + [pltpu.make_async_copy(at_tile(w_ref, part * steps + j, t), wv.at[j], sems.at[j]) for j in range(steps)]


def forward_kernel(n, cols, part, emit, place_ref, *refs):
    x_refs, (w_ref, keep_ref) = refs[:cols], refs[cols : cols + 2]
    outs, (xs, wv, kv, ov, w_sems, o_sems, x_sem) = refs[cols + 2 : -7], refs[-7:]
    steps, _, t = wv.shape
    tokens = xs.shape[0]
    half = tokens // 2
    for k, at, held, size in token_places(n, cols, tokens, place_ref):
        pltpu.make_async_copy(x_refs[k].at[pl.ds(at, size), :], xs.at[pl.ds(held, size), :], x_sem).start()
    loads = load_weight(w_ref, keep_ref, wv, kv, w_sems, part)
    for copy in loads[: 1 + AHEAD]:
        copy.start()
    pltpu.make_async_copy(xs, xs, x_sem).wait()
    stores = []
    if emit:
        stores.append(pltpu.make_async_copy(xs, outs[2], x_sem))
        stores[0].start()
    loads[0].wait()
    for j in range(steps):
        loads[1 + j].wait()
        if j + AHEAD < steps:
            loads[1 + j + AHEAD].start()
        mask_tile(wv.at[j], kv[:, j * t : (j + 1) * t])
        acc = jnp.dot(xs[...], wv[j], preferred_element_type=jnp.float32)
        ov[j] = acc.astype(jnp.bfloat16)
        for i in range(2):
            rows = pl.ds(i * half, half)
            stores.append(pltpu.make_async_copy(ov.at[j, rows, :], at_tile(outs[i], j, t), o_sems.at[i, j]))
            stores[-1].start()
    for copy in stores:
        copy.wait()


ANY = pl.BlockSpec(memory_space=pl.ANY)


def call(kernel, name, place, args, out_shape, scratch, aliases=None, after=(), cost=COST):
    held = len(args)
    body = lambda place_ref, *refs: kernel(place_ref, *refs[:held], *refs[held + len(after) :])
    return pl.pallas_call(
        body,
        grid_spec=pltpu.PrefetchScalarGridSpec(
            num_scalar_prefetch=1,
            grid=(),
            in_specs=[ANY] * (held + len(after)),
            out_specs=jax.tree.map(lambda _: ANY, out_shape),
            scratch_shapes=scratch,
        ),
        out_shape=out_shape,
        input_output_aliases=aliases or {},
        compiler_params=pltpu.CompilerParams(vmem_limit_bytes=VMEM_LIMIT),
        cost_estimate=pl.CostEstimate(flops=cost, bytes_accessed=cost, transcendentals=0),
        name=name,
    )(place, *args, *after)


def pause_kernel(place_ref, out_ref, held, sem):
    held[...] = jnp.zeros_like(held)
    store = pltpu.make_async_copy(held, out_ref, sem)
    store.start()
    store.wait()


def pause(place, after):
    shape = (8, 128)
    return call(
        pause_kernel,
        "pause",
        place,
        [],
        jax.ShapeDtypeStruct(shape, jnp.float32),
        [pltpu.VMEM(shape, jnp.float32), pltpu.SemaphoreType.DMA],
        after=after,
    )


def forward(place, xs, weight, keep, after, part, n, emit):
    depth, width = weight.shape
    t = tile_of(width // PARTS)
    steps = width // PARTS // t
    tokens = xs[0].shape[0] * len(xs)
    bf16 = jnp.bfloat16
    outs = [jax.ShapeDtypeStruct((tokens // 2, steps * t), bf16)] * 2
    return call(
        functools.partial(forward_kernel, n, len(xs), part, emit),
        "forward",
        place,
        [*xs, weight, keep],
        outs + ([jax.ShapeDtypeStruct((tokens, depth), bf16)] if emit else []),
        [
            pltpu.VMEM((tokens, depth), bf16),
            pltpu.VMEM((steps, depth, t), bf16),
            pltpu.VMEM((depth // BLOCK, steps * t), jnp.float32),
            pltpu.VMEM((steps, tokens, t), bf16),
            pltpu.SemaphoreType.DMA((steps + 1,)),
            pltpu.SemaphoreType.DMA((2, steps)),
            pltpu.SemaphoreType.DMA,
        ],
        after=after,
        cost=COST if part else 1,
    )


def origin_of(n, z, piece):
    link, s, _ = piece
    sign = jnp.where(z % 2 == 0, s, -s)
    if link == 2:
        return jnp.where((z + sign >= 0) & (z + sign < n), z + sign, z - sign)
    return z - sign if link == 1 else z + sign


def groups_of(steps):
    ends = sorted({min(e, steps) for e in (1, 4, steps)})
    return list(zip([0, *ends], ends))


def start_pieces(n, place_ref, pieces, refs, held, sems, t):
    tokens, width = held.shape
    tr = tokens // (2 * n)
    for g, (lo, hi) in enumerate(groups_of(width // t)):
        for piece, ref in zip(pieces, refs):
            origin = origin_of(n, place_ref[0], piece)

            @pl.when((origin >= 0) & (origin < n))
            def _():
                at = pl.multiple_of(piece[2] * (tokens // 2) + origin * tr, tr)
                columns = pl.ds(lo * t, (hi - lo) * t)
                pltpu.make_async_copy(ref.at[:, columns], held.at[pl.ds(at, tr), columns], sems.at[g]).start()


def each_piece(n, place_ref, pieces, body):
    for i, piece in enumerate(pieces):
        origin = origin_of(n, place_ref[0], piece)
        pl.when((origin >= 0) & (origin < n))(functools.partial(body, i, origin))


def product_rows(n, place_ref, pieces, piece_refs, w_ref, keep_ref, held, wv, kv, acc, sems, w_sems):
    steps, _, t = wv.shape
    tr = held.shape[0] // len(pieces)
    loads = load_weight(w_ref, keep_ref, wv, kv, w_sems, 0)
    for copy in loads[:2]:
        copy.start()

    def rows_of(i):
        return pltpu.make_async_copy(piece_refs[i], held.at[pl.ds(i * tr, tr), :], sems.at[i])

    each_piece(n, place_ref, pieces, lambda i, _: rows_of(i).start())
    for copy in loads[2 : 1 + ROWS_AHEAD]:
        copy.start()
    each_piece(n, place_ref, pieces, lambda i, _: rows_of(i).wait())
    loads[0].wait()
    for j in range(steps):
        loads[1 + j].wait()
        if j + ROWS_AHEAD < steps:
            loads[1 + j + ROWS_AHEAD].start()
        columns = slice(j * t, (j + 1) * t)
        mask_tile(wv.at[j], kv[:, columns])
        product = lax.dot_general(held[:, columns], wv[j], (((1,), (1,)), ((), ())), preferred_element_type=jnp.float32)
        if j == 0:
            acc[...] = product
        else:
            acc[...] += product


def early_kernel(n, pieces, place_ref, *refs):
    piece_refs, (w_ref, keep_ref, out_ref, held, wv, kv, acc, ob, sems, w_sems, o_sem) = refs[: len(pieces)], refs[len(pieces) :]
    product_rows(n, place_ref, pieces, piece_refs, w_ref, keep_ref, held, wv, kv, acc, sems, w_sems)
    ob[...] = acc[...].astype(jnp.bfloat16)
    store = pltpu.make_async_copy(ob, out_ref, o_sem)
    store.start()
    store.wait()


def early_rows(place, n, pieces, arrays, weight, keep, after):
    depth, width = weight.shape
    t = tile_of(width // PARTS)
    steps = width // t
    rows = len(pieces) * arrays[0].shape[0]
    f32, bf16 = jnp.float32, jnp.bfloat16
    return call(
        functools.partial(early_kernel, n, pieces),
        "early_rows",
        place,
        [*arrays, weight, keep],
        jax.ShapeDtypeStruct((rows, depth), bf16),
        [
            pltpu.VMEM((rows, width), bf16),
            pltpu.VMEM((steps, depth, t), bf16),
            pltpu.VMEM((depth // BLOCK, width), f32),
            pltpu.VMEM((rows, depth), f32),
            pltpu.VMEM((rows, depth), bf16),
            pltpu.SemaphoreType.DMA((len(pieces),)),
            pltpu.SemaphoreType.DMA((steps + 1,)),
            pltpu.SemaphoreType.DMA,
        ],
        after=after,
    )


def late_kernel(n, cols, early, late, place_ref, *refs):
    piece_refs, (w_ref, keep_ref, early_ref), refs = refs[: len(late)], refs[len(late) : len(late) + 3], refs[len(late) + 3 :]
    out_refs, (held, wv, kv, acc, ob, sems, w_sems, e_sems, o_sem) = refs[:cols], refs[cols:]
    tokens = ob.shape[0]
    tr = tokens // (2 * n)
    rows = lambda piece, origin: pl.ds(pl.multiple_of(piece[2] * (tokens // 2) + origin * tr, tr), tr)

    def early_of(i, origin):
        return pltpu.make_async_copy(early_ref.at[pl.ds(i * tr, tr), :], ob.at[rows(early[i], origin), :], e_sems.at[i])

    each_piece(n, place_ref, early, lambda i, origin: early_of(i, origin).start())
    product_rows(n, place_ref, late, piece_refs, w_ref, keep_ref, held, wv, kv, acc, sems, w_sems)
    each_piece(n, place_ref, early, lambda i, origin: early_of(i, origin).wait())

    def store(i, origin):
        ob[rows(late[i], origin), :] = acc[i * tr : (i + 1) * tr, :].astype(jnp.bfloat16)

    each_piece(n, place_ref, late, store)
    for k, at, row, size in token_places(n, cols, tokens, place_ref):
        pltpu.make_async_copy(ob.at[pl.ds(row, size), :], out_refs[k].at[pl.ds(at, size), :], o_sem).start()
    pltpu.make_async_copy(ob, ob, o_sem).wait()


def late_rows(place, early, late, arrays, weight, keep, done, after, n, cols):
    depth, width = weight.shape
    tr = arrays[0].shape[0]
    tokens = 2 * n * tr
    t = tile_of(width // PARTS)
    steps = width // t
    f32, bf16 = jnp.float32, jnp.bfloat16
    rows = len(late) * tr
    return call(
        functools.partial(late_kernel, n, cols, early, late),
        "late_rows",
        place,
        [*arrays, weight, keep, done],
        [jax.ShapeDtypeStruct((tokens // cols, depth), bf16)] * cols,
        [
            pltpu.VMEM((rows, width), bf16),
            pltpu.VMEM((steps, depth, t), bf16),
            pltpu.VMEM((depth // BLOCK, width), f32),
            pltpu.VMEM((rows, depth), f32),
            pltpu.VMEM((tokens, depth), bf16),
            pltpu.SemaphoreType.DMA((len(late),)),
            pltpu.SemaphoreType.DMA((steps + 1,)),
            pltpu.SemaphoreType.DMA((len(early),)),
            pltpu.SemaphoreType.DMA,
        ],
        after=after,
    )


def send_kernel(n, k, links, behind, place_ref, *refs):
    mine_ref, theirs_ref, refs = refs[0], refs[1], refs[2:]
    came_refs, refs = refs[: len(behind)], refs[len(behind) :]
    out_refs, (terms, cv, ov, sems, o_sems) = refs[: len(links)], refs[len(links) :]
    tr = ov.shape[1]
    z = place_ref[0]
    odd = lax.rem(z, 2)

    def each_link(body):
        for i, link in enumerate(links):
            upward = odd == link
            d = jnp.where(upward, z + n - k + 1, z - n + k - 1)
            pl.when((d >= 0) & (d < n))(functools.partial(body, i, link, d))

    def load(i, link, d):
        for h, ref in enumerate((mine_ref, theirs_ref)):
            source = ref.at[pl.ds(pl.multiple_of(d * tr, tr), tr), :]
            pltpu.make_async_copy(source, terms.at[i, h], sems.at[i]).start()
        if 1 - link in behind:
            pltpu.make_async_copy(came_refs[behind.index(1 - link)], cv.at[i], sems.at[len(links) + i]).start()

    def add(i, link, d):
        pltpu.make_async_copy(terms.at[i], terms.at[i], sems.at[i]).wait()
        total = terms[i, 0].astype(jnp.float32) + terms[i, 1].astype(jnp.float32)
        if 1 - link in behind:
            pltpu.make_async_copy(cv.at[i], cv.at[i], sems.at[len(links) + i]).wait()
            other = z + 1 - 2 * odd if link == 1 else z - 1 + 2 * odd
            total += jnp.where((other >= 0) & (other < n), cv[i].astype(jnp.float32), 0.0)
        ov[i] = total.astype(jnp.bfloat16)
        pltpu.make_async_copy(ov.at[i], out_refs[i], o_sems.at[i]).start()

    each_link(load)
    each_link(add)
    each_link(lambda i, link, d: pltpu.make_async_copy(ov.at[i], out_refs[i], o_sems.at[i]).wait())


def send_sums(place, mine, theirs, came, links, after, k, n, first):
    behind = tuple(link for link in range(2) if came[link] is not None)
    pw = mine.shape[1]
    tr = mine.shape[0] // n
    bf16 = jnp.bfloat16
    return call(
        functools.partial(send_kernel, n, k, links, behind),
        "send_sums",
        place,
        [mine, theirs, *(came[link] for link in behind)],
        [jax.ShapeDtypeStruct((tr, pw), bf16)] * len(links),
        [
            pltpu.VMEM((len(links), 2, tr, pw), bf16),
            pltpu.VMEM((len(links), tr, pw), bf16),
            pltpu.VMEM((len(links), tr, pw), bf16),
            pltpu.SemaphoreType.DMA((2 * len(links),)),
            pltpu.SemaphoreType.DMA((len(links),)),
        ],
        after=after,
        cost=COST if k == n and first else 1,
    )


def weight_grad_kernel(n, pieces, scale, place_ref, *refs):
    piece_refs, (xt_ref, keep_ref, out_ref, held, xt, kv, ov, sems, x_sems, o_sems) = refs[: len(pieces)], refs[len(pieces) :]
    steps, _, t = ov.shape
    loads = [pltpu.make_async_copy(xt_ref, xt, x_sems.at[0]), pltpu.make_async_copy(keep_ref, kv, x_sems.at[1])]
    for copy in loads:
        copy.start()
    start_pieces(n, place_ref, pieces, piece_refs, held, sems, t)
    groups = groups_of(steps)
    for copy in loads:
        copy.wait()
    stores = []
    for j in range(steps):
        for g, (lo, hi) in enumerate(groups):
            if lo == j:
                part = held.at[:, pl.ds(lo * t, (hi - lo) * t)]
                pltpu.make_async_copy(part, part, sems.at[g]).wait()
        acc = jnp.dot(xt[...], held[:, j * t : (j + 1) * t], preferred_element_type=jnp.float32)
        for a in range(xt.shape[0] // BLOCK):
            rows = slice(a * BLOCK, (a + 1) * BLOCK)
            keep = kv[a : a + 1, j * t : (j + 1) * t] * scale
            ov[j, rows, :] = (acc[rows, :] * keep).astype(jnp.bfloat16)
        stores.append(pltpu.make_async_copy(ov.at[j], at_tile(out_ref, j, t), o_sems.at[j]))
        stores[-1].start()
    for copy in stores:
        copy.wait()


def weight_grad(place, pieces, arrays, xt, keep, n, width):
    depth, tokens = xt.shape
    t = tile_of(width // PARTS)
    steps = width // t
    bf16 = jnp.bfloat16
    return call(
        functools.partial(weight_grad_kernel, n, pieces, tokens ** (-0.5)),
        "weight_grad",
        place,
        [*arrays, xt, keep],
        jax.ShapeDtypeStruct((depth, width), bf16),
        [
            pltpu.VMEM((tokens, width), bf16),
            pltpu.VMEM((depth, tokens), bf16),
            pltpu.VMEM((depth // BLOCK, width), jnp.float32),
            pltpu.VMEM((steps, depth, t), bf16),
            pltpu.SemaphoreType.DMA((len(groups_of(steps)),)),
            pltpu.SemaphoreType.DMA((2,)),
            pltpu.SemaphoreType.DMA((steps,)),
        ],
    )


def finish_kernel(n, cols, links, place_ref, *refs):
    z = place_ref[0]
    each = 2 + len(links)
    sum_refs, grad_refs, (out_ref, grad_ref, sv, gv, ov, ob, sems, o_sems) = (
        refs[: each * PARTS],
        refs[each * PARTS : each * PARTS + cols],
        refs[each * PARTS + cols :],
    )
    tr, pw = sv.shape[-2:]
    for p in range(PARTS):
        for i in range(each):
            ref = sum_refs[each * p + i]
            if i < 2:
                ref = ref.at[pl.ds(pl.multiple_of(z * tr, tr), tr), :]
            pltpu.make_async_copy(ref, sv.at[p, i], sems.at[p]).start()
    for k in range(cols):
        pltpu.make_async_copy(grad_refs[k], gv.at[k], sems.at[PARTS]).start()
    odd = lax.rem(z, 2)
    stores = []
    for p in range(PARTS):
        pltpu.make_async_copy(sv.at[p], sv.at[p], sems.at[p]).wait()
        total = sv[p, 0].astype(jnp.float32) + sv[p, 1].astype(jnp.float32)
        for i, link in enumerate(links):
            other = z + 1 - 2 * odd if link == 0 else z - 1 + 2 * odd
            came = sv[p, 2 + i].astype(jnp.float32)
            total += jnp.where((other >= 0) & (other < n), came, 0.0)
        ov[p] = total.astype(jnp.bfloat16)
        stores.append(pltpu.make_async_copy(ov.at[p], out_ref.at[:, pl.ds(p * pw, pw)], o_sems.at[p]))
        stores[-1].start()
    pltpu.make_async_copy(gv, gv, sems.at[PARTS]).wait()
    total = gv[0].astype(jnp.float32)
    for k in range(1, cols):
        total += gv[k].astype(jnp.float32)
    ob[...] = total.astype(jnp.bfloat16)
    stores.append(pltpu.make_async_copy(ob, grad_ref, o_sems.at[PARTS]))
    stores[-1].start()
    for copy in stores:
        copy.wait()


def finish(place, sums, grads, links, n):
    tr, pw = sums[0][-1].shape
    rows, depth = grads[0].shape
    cols = len(grads)
    bf16 = jnp.bfloat16
    return call(
        functools.partial(finish_kernel, n, cols, links),
        "finish",
        place,
        [v for part in sums for v in part] + grads,
        [jax.ShapeDtypeStruct((tr, pw * PARTS), bf16), jax.ShapeDtypeStruct((rows, depth), bf16)],
        [
            pltpu.VMEM((PARTS, 2 + len(links), tr, pw), bf16),
            pltpu.VMEM((cols, rows, depth), bf16),
            pltpu.VMEM((PARTS, tr, pw), bf16),
            pltpu.VMEM((rows, depth), bf16),
            pltpu.SemaphoreType.DMA((PARTS + 1,)),
            pltpu.SemaphoreType.DMA((PARTS + 1,)),
        ],
    )


def local(n, cols, inputs, weight, mask, cotangent):
    row, col = lax.axis_index("row"), lax.axis_index("col")
    z, core = row // 2, row % 2
    place = jnp.stack([z, core, col]).astype(jnp.int32)
    width = weight.shape[1]
    pw = width // PARTS
    tr = cotangent.shape[0]
    tokens = tr * 2 * n

    f32, bf16 = jnp.float32, jnp.bfloat16
    swap = lambda v: lax.ppermute(v, "row", [(i, i ^ 1) for i in range(2 * n)])
    across = lambda v, k: lax.ppermute(v, "col", [(i, i ^ k) for i in range(cols)])

    def pairs_of(link, ups, downs):
        pairs = [(i, i + 1) for i in ups if i % 2 == link and i + 1 < n]
        return pairs + [(i, i - 1) for i in downs if i % 2 != link and i > 0]

    def over(v, link, ups, downs):
        pairs = pairs_of(link, ups, downs)
        if not pairs:
            return None
        pairs = [(2 * i + c, 2 * j + c) for i, j in pairs for c in range(2)]
        if {i for i, _ in pairs} == {j for _, j in pairs}:
            pairs += [(i, i ^ 1) for i in sorted(set(range(2 * n)) - {i for i, _ in pairs})]
        return lax.ppermute(v, "row", pairs)

    even = z % 2 == 0

    xs = [inputs] + [across(inputs, k) for k in range(1, cols)]
    keep = jnp.repeat(mask.astype(f32), BLOCK, axis=1)
    came = [over(cotangent, link, range(n), range(n)) for link in range(2)]
    first = came
    pieces = [((0, 0, 0), cotangent), ((0, 0, 1), swap(cotangent))]

    def keep_pieces(s):
        have = [(link, v) for link, v in enumerate(came) if v is not None]
        if len(have) == 2 and 2 * s >= n:
            origin = jnp.where(even, z + s, z - s)
            have = [(2, jnp.where((origin >= 0) & (origin < n), *came))]
        for link, v in have:
            pieces.extend([((link, s, 0), v), ((link, s, 1), swap(v))])

    keep_pieces(1)

    mine, theirs = [], []
    for p in range(PARTS):
        m, other, *more = forward(place, xs, weight, keep, first if p else (), p, n, p == 0)
        whole = more[0] if more else whole
        mine.append(m)
        theirs.append(swap(other))
    xt = whole.T

    sums = [[None, None] for _ in range(PARTS)]
    sent = {}

    def slot(k, p, after):
        ups, downs = range(k - 1), range(n - k + 1, n)
        links = tuple(link for link in range(2) if pairs_of(link, ups, downs))
        sent[k, p] = send_sums(place, mine[p], theirs[p], sums[p], links, after, k, n, p == 0)
        sums[p] = [None, None]
        for link, v in zip(links, sent[k, p]):
            sums[p][link] = over(v, link, ups, downs)

    after = ()
    for k in range(2, n + 1):
        if k < n:
            came = [
                None if came[1 - link] is None else over(came[1 - link], link, range(k - 1, n), range(n - k + 1))
                for link in range(2)
            ]
        slot(k, 0, after)
        after = sent[k, 0]
        if k == 2:
            held = [(i, v) for i, v in pieces if 2 * i[1] < n]
            kinds = [i for i, _ in held]
            early = early_rows(place, n, kinds, [v for _, v in held], weight, keep, after)
            came, after = lax.optimization_barrier((came, [early]))
            after = [*after, *(v for v in came if v is not None)]
        if k == n:
            late = [(i, v) for i, v in pieces if 2 * i[1] >= n]
            parts = late_rows(
                place, kinds, [i for i, _ in late], [v for _, v in late], weight, keep, early, after, n, cols
            )
            after = parts
        for p in range(1, PARTS):
            slot(k, p, after)
            after = sent[k, p]
        if 2 < k < n:
            after = [pause(place, after)]
            came, after = lax.optimization_barrier((came, after))
        if k < n:
            keep_pieces(k)
    grads = [parts[0]] + [across(parts[k], k) for k in range(1, cols)]
    wg = weight_grad(place, [k for k, _ in pieces], [v for _, v in pieces], xt, keep, n, width)
    links = [link for link in range(2) if sums[0][link] is not None]
    ends = [[mine[p], theirs[p], *(sums[p][link] for link in links)] for p in range(PARTS)]
    outputs, input_grad = finish(place, ends, grads, links, n)
    return outputs, input_grad, wg


def solution(mesh):
    n, cols = mesh.shape["row"] // 2, mesh.shape["col"]
    return jax.shard_map(
        functools.partial(local, n, cols),
        mesh=mesh,
        in_specs=(P("col", "row"), P("row", "col"), P("row", "col"), P("row", "col")),
        out_specs=(P("row", "col"), P("col", "row"), P("row", "col")),
        check_vma=False,
    )
```

```python
import functools

import jax
import jax.numpy as jnp
from jax import lax
from jax.experimental import pallas as pl
from jax.experimental.pallas import tpu as pltpu
from jax.sharding import PartitionSpec as P

BLOCK = 128
PARTS = 2
AHEAD = 2
ROWS_AHEAD = 4
COST = 10 ** 11
VMEM_LIMIT = 64 * 1024 * 1024


def tile_of(width):
    return next(t for t in (512, 256, 128) if width % t == 0)


def at_tile(ref, j, t):
    return ref.at[:, pl.ds(j * t, t)]


def token_places(n, cols, tokens, place_ref):
    own, tr = tokens // cols, tokens // (2 * n)
    size = min(own, tr)
    for k in range(cols):
        for i in range(own // size):
            row = (place_ref[2] ^ k) * own + i * size
            r = row // tr
            held = ((r + place_ref[1]) % 2) * (tokens // 2) + (r // 2) * tr + row % tr
            yield k, i * size, pl.multiple_of(held, size), size


def mask_tile(tile_ref, keep):
    for a in range(tile_ref.shape[0] // BLOCK):
        rows = slice(a * BLOCK, (a + 1) * BLOCK)
        tile_ref[rows, :] = tile_ref[rows, :] * keep[a : a + 1, :].astype(tile_ref.dtype)


def load_weight(w_ref, keep_ref, wv, kv, sems, part):
    steps, _, t = wv.shape
    copies = [pltpu.make_async_copy(keep_ref.at[:, pl.ds(part * steps * t, steps * t)], kv, sems.at[steps])]
    return copies + [pltpu.make_async_copy(at_tile(w_ref, part * steps + j, t), wv.at[j], sems.at[j]) for j in range(steps)]


def forward_kernel(n, cols, part, emit, place_ref, *refs):
    x_refs, (w_ref, keep_ref) = refs[:cols], refs[cols : cols + 2]
    outs, (xs, wv, kv, ov, w_sems, o_sems, x_sem) = refs[cols + 2 : -7], refs[-7:]
    steps, _, t = wv.shape
    tokens = xs.shape[0]
    half = tokens // 2
    for k, at, held, size in token_places(n, cols, tokens, place_ref):
        pltpu.make_async_copy(x_refs[k].at[pl.ds(at, size), :], xs.at[pl.ds(held, size), :], x_sem).start()
    loads = load_weight(w_ref, keep_ref, wv, kv, w_sems, part)
    for copy in loads[: 1 + AHEAD]:
        copy.start()
    pltpu.make_async_copy(xs, xs, x_sem).wait()
    stores = []
    if emit:
        stores.append(pltpu.make_async_copy(xs, outs[2], x_sem))
        stores[0].start()
    loads[0].wait()
    for j in range(steps):
        loads[1 + j].wait()
        if j + AHEAD < steps:
            loads[1 + j + AHEAD].start()
        mask_tile(wv.at[j], kv[:, j * t : (j + 1) * t])
        acc = jnp.dot(xs[...], wv[j], preferred_element_type=jnp.float32)
        ov[j] = acc.astype(jnp.bfloat16)
        for i in range(2):
            rows = pl.ds(i * half, half)
            stores.append(pltpu.make_async_copy(ov.at[j, rows, :], at_tile(outs[i], j, t), o_sems.at[i, j]))
            stores[-1].start()
    for copy in stores:
        copy.wait()


ANY = pl.BlockSpec(memory_space=pl.ANY)


def call(kernel, name, place, args, out_shape, scratch, aliases=None, after=(), cost=COST):
    held = len(args)
    body = lambda place_ref, *refs: kernel(place_ref, *refs[:held], *refs[held + len(after) :])
    return pl.pallas_call(
        body,
        grid_spec=pltpu.PrefetchScalarGridSpec(
            num_scalar_prefetch=1,
            grid=(),
            in_specs=[ANY] * (held + len(after)),
            out_specs=jax.tree.map(lambda _: ANY, out_shape),
            scratch_shapes=scratch,
        ),
        out_shape=out_shape,
        input_output_aliases=aliases or {},
        compiler_params=pltpu.CompilerParams(vmem_limit_bytes=VMEM_LIMIT),
        cost_estimate=pl.CostEstimate(flops=cost, bytes_accessed=cost, transcendentals=0),
        name=name,
    )(place, *args, *after)


def forward(place, xs, weight, keep, after, part, n, emit):
    depth, width = weight.shape
    t = tile_of(width // PARTS)
    steps = width // PARTS // t
    tokens = xs[0].shape[0] * len(xs)
    bf16 = jnp.bfloat16
    outs = [jax.ShapeDtypeStruct((tokens // 2, steps * t), bf16)] * 2
    return call(
        functools.partial(forward_kernel, n, len(xs), part, emit),
        "forward",
        place,
        [*xs, weight, keep],
        outs + ([jax.ShapeDtypeStruct((tokens, depth), bf16)] if emit else []),
        [
            pltpu.VMEM((tokens, depth), bf16),
            pltpu.VMEM((steps, depth, t), bf16),
            pltpu.VMEM((depth // BLOCK, steps * t), jnp.float32),
            pltpu.VMEM((steps, tokens, t), bf16),
            pltpu.SemaphoreType.DMA((steps + 1,)),
            pltpu.SemaphoreType.DMA((2, steps)),
            pltpu.SemaphoreType.DMA,
        ],
        after=after,
        cost=COST if part else 1,
    )


def origin_of(n, z, piece):
    link, s, _ = piece
    sign = jnp.where(z % 2 == 0, s, -s)
    if link == 2:
        return jnp.where((z + sign >= 0) & (z + sign < n), z + sign, z - sign)
    return z - sign if link == 1 else z + sign


def groups_of(steps):
    ends = sorted({min(e, steps) for e in (1, 4, steps)})
    return list(zip([0, *ends], ends))


def start_pieces(n, place_ref, pieces, refs, held, sems, t):
    tokens, width = held.shape
    tr = tokens // (2 * n)
    for g, (lo, hi) in enumerate(groups_of(width // t)):
        for piece, ref in zip(pieces, refs):
            origin = origin_of(n, place_ref[0], piece)

            @pl.when((origin >= 0) & (origin < n))
            def _():
                at = pl.multiple_of(piece[2] * (tokens // 2) + origin * tr, tr)
                columns = pl.ds(lo * t, (hi - lo) * t)
                pltpu.make_async_copy(ref.at[:, columns], held.at[pl.ds(at, tr), columns], sems.at[g]).start()


def each_piece(n, place_ref, pieces, body):
    for i, piece in enumerate(pieces):
        origin = origin_of(n, place_ref[0], piece)
        pl.when((origin >= 0) & (origin < n))(functools.partial(body, i, origin))


def product_rows(n, place_ref, pieces, piece_refs, w_ref, keep_ref, held, wv, kv, acc, sems, w_sems):
    steps, _, t = wv.shape
    tr = held.shape[0] // len(pieces)
    loads = load_weight(w_ref, keep_ref, wv, kv, w_sems, 0)
    for copy in loads[:2]:
        copy.start()

    def rows_of(i):
        return pltpu.make_async_copy(piece_refs[i], held.at[pl.ds(i * tr, tr), :], sems.at[i])

    each_piece(n, place_ref, pieces, lambda i, _: rows_of(i).start())
    for copy in loads[2 : 1 + ROWS_AHEAD]:
        copy.start()
    each_piece(n, place_ref, pieces, lambda i, _: rows_of(i).wait())
    loads[0].wait()
    for j in range(steps):
        loads[1 + j].wait()
        if j + ROWS_AHEAD < steps:
            loads[1 + j + ROWS_AHEAD].start()
        columns = slice(j * t, (j + 1) * t)
        mask_tile(wv.at[j], kv[:, columns])
        product = lax.dot_general(held[:, columns], wv[j], (((1,), (1,)), ((), ())), preferred_element_type=jnp.float32)
        if j == 0:
            acc[...] = product
        else:
            acc[...] += product


def early_kernel(n, pieces, place_ref, *refs):
    piece_refs, (w_ref, keep_ref, out_ref, held, wv, kv, acc, ob, sems, w_sems, o_sem) = refs[: len(pieces)], refs[len(pieces) :]
    product_rows(n, place_ref, pieces, piece_refs, w_ref, keep_ref, held, wv, kv, acc, sems, w_sems)
    ob[...] = acc[...].astype(jnp.bfloat16)
    store = pltpu.make_async_copy(ob, out_ref, o_sem)
    store.start()
    store.wait()


def early_rows(place, n, pieces, arrays, weight, keep, after):
    depth, width = weight.shape
    t = tile_of(width // PARTS)
    steps = width // t
    rows = len(pieces) * arrays[0].shape[0]
    f32, bf16 = jnp.float32, jnp.bfloat16
    return call(
        functools.partial(early_kernel, n, pieces),
        "early_rows",
        place,
        [*arrays, weight, keep],
        jax.ShapeDtypeStruct((rows, depth), bf16),
        [
            pltpu.VMEM((rows, width), bf16),
            pltpu.VMEM((steps, depth, t), bf16),
            pltpu.VMEM((depth // BLOCK, width), f32),
            pltpu.VMEM((rows, depth), f32),
            pltpu.VMEM((rows, depth), bf16),
            pltpu.SemaphoreType.DMA((len(pieces),)),
            pltpu.SemaphoreType.DMA((steps + 1,)),
            pltpu.SemaphoreType.DMA,
        ],
        after=after,
    )


def late_kernel(n, cols, early, late, place_ref, *refs):
    piece_refs, (w_ref, keep_ref, early_ref), refs = refs[: len(late)], refs[len(late) : len(late) + 3], refs[len(late) + 3 :]
    out_refs, (held, wv, kv, acc, ob, sems, w_sems, e_sems, o_sem) = refs[:cols], refs[cols:]
    tokens = ob.shape[0]
    tr = tokens // (2 * n)
    rows = lambda piece, origin: pl.ds(pl.multiple_of(piece[2] * (tokens // 2) + origin * tr, tr), tr)

    def early_of(i, origin):
        return pltpu.make_async_copy(early_ref.at[pl.ds(i * tr, tr), :], ob.at[rows(early[i], origin), :], e_sems.at[i])

    each_piece(n, place_ref, early, lambda i, origin: early_of(i, origin).start())
    product_rows(n, place_ref, late, piece_refs, w_ref, keep_ref, held, wv, kv, acc, sems, w_sems)
    each_piece(n, place_ref, early, lambda i, origin: early_of(i, origin).wait())

    def store(i, origin):
        ob[rows(late[i], origin), :] = acc[i * tr : (i + 1) * tr, :].astype(jnp.bfloat16)

    each_piece(n, place_ref, late, store)
    for k, at, row, size in token_places(n, cols, tokens, place_ref):
        pltpu.make_async_copy(ob.at[pl.ds(row, size), :], out_refs[k].at[pl.ds(at, size), :], o_sem).start()
    pltpu.make_async_copy(ob, ob, o_sem).wait()


def late_rows(place, early, late, arrays, weight, keep, done, after, n, cols):
    depth, width = weight.shape
    tr = arrays[0].shape[0]
    tokens = 2 * n * tr
    t = tile_of(width // PARTS)
    steps = width // t
    f32, bf16 = jnp.float32, jnp.bfloat16
    rows = len(late) * tr
    return call(
        functools.partial(late_kernel, n, cols, early, late),
        "late_rows",
        place,
        [*arrays, weight, keep, done],
        [jax.ShapeDtypeStruct((tokens // cols, depth), bf16)] * cols,
        [
            pltpu.VMEM((rows, width), bf16),
            pltpu.VMEM((steps, depth, t), bf16),
            pltpu.VMEM((depth // BLOCK, width), f32),
            pltpu.VMEM((rows, depth), f32),
            pltpu.VMEM((tokens, depth), bf16),
            pltpu.SemaphoreType.DMA((len(late),)),
            pltpu.SemaphoreType.DMA((steps + 1,)),
            pltpu.SemaphoreType.DMA((len(early),)),
            pltpu.SemaphoreType.DMA,
        ],
        after=after,
    )


def send_kernel(n, k, links, behind, place_ref, *refs):
    mine_ref, theirs_ref, refs = refs[0], refs[1], refs[2:]
    came_refs, refs = refs[: len(behind)], refs[len(behind) :]
    out_refs, (terms, cv, ov, sems, o_sems) = refs[: len(links)], refs[len(links) :]
    tr = ov.shape[1]
    z = place_ref[0]
    odd = lax.rem(z, 2)

    def each_link(body):
        for i, link in enumerate(links):
            upward = odd == link
            d = jnp.where(upward, z + n - k + 1, z - n + k - 1)
            pl.when((d >= 0) & (d < n))(functools.partial(body, i, link, d))

    def load(i, link, d):
        for h, ref in enumerate((mine_ref, theirs_ref)):
            source = ref.at[pl.ds(pl.multiple_of(d * tr, tr), tr), :]
            pltpu.make_async_copy(source, terms.at[i, h], sems.at[i]).start()
        if 1 - link in behind:
            pltpu.make_async_copy(came_refs[behind.index(1 - link)], cv.at[i], sems.at[len(links) + i]).start()

    def add(i, link, d):
        pltpu.make_async_copy(terms.at[i], terms.at[i], sems.at[i]).wait()
        total = terms[i, 0].astype(jnp.float32) + terms[i, 1].astype(jnp.float32)
        if 1 - link in behind:
            pltpu.make_async_copy(cv.at[i], cv.at[i], sems.at[len(links) + i]).wait()
            other = z + 1 - 2 * odd if link == 1 else z - 1 + 2 * odd
            total += jnp.where((other >= 0) & (other < n), cv[i].astype(jnp.float32), 0.0)
        ov[i] = total.astype(jnp.bfloat16)
        pltpu.make_async_copy(ov.at[i], out_refs[i], o_sems.at[i]).start()

    each_link(load)
    each_link(add)
    each_link(lambda i, link, d: pltpu.make_async_copy(ov.at[i], out_refs[i], o_sems.at[i]).wait())


def send_sums(place, mine, theirs, came, links, after, k, n, first):
    behind = tuple(link for link in range(2) if came[link] is not None)
    pw = mine.shape[1]
    tr = mine.shape[0] // n
    bf16 = jnp.bfloat16
    return call(
        functools.partial(send_kernel, n, k, links, behind),
        "send_sums",
        place,
        [mine, theirs, *(came[link] for link in behind)],
        [jax.ShapeDtypeStruct((tr, pw), bf16)] * len(links),
        [
            pltpu.VMEM((len(links), 2, tr, pw), bf16),
            pltpu.VMEM((len(links), tr, pw), bf16),
            pltpu.VMEM((len(links), tr, pw), bf16),
            pltpu.SemaphoreType.DMA((2 * len(links),)),
            pltpu.SemaphoreType.DMA((len(links),)),
        ],
        after=after,
        cost=COST if k == n and first else 1,
    )


def weight_grad_kernel(n, pieces, scale, place_ref, *refs):
    piece_refs, (xt_ref, keep_ref, out_ref, held, xt, kv, ov, sems, x_sems, o_sems) = refs[: len(pieces)], refs[len(pieces) :]
    steps, _, t = ov.shape
    loads = [pltpu.make_async_copy(xt_ref, xt, x_sems.at[0]), pltpu.make_async_copy(keep_ref, kv, x_sems.at[1])]
    for copy in loads:
        copy.start()
    start_pieces(n, place_ref, pieces, piece_refs, held, sems, t)
    groups = groups_of(steps)
    for copy in loads:
        copy.wait()
    stores = []
    for j in range(steps):
        for g, (lo, hi) in enumerate(groups):
            if lo == j:
                part = held.at[:, pl.ds(lo * t, (hi - lo) * t)]
                pltpu.make_async_copy(part, part, sems.at[g]).wait()
        acc = jnp.dot(xt[...], held[:, j * t : (j + 1) * t], preferred_element_type=jnp.float32)
        for a in range(xt.shape[0] // BLOCK):
            rows = slice(a * BLOCK, (a + 1) * BLOCK)
            keep = kv[a : a + 1, j * t : (j + 1) * t] * scale
            ov[j, rows, :] = (acc[rows, :] * keep).astype(jnp.bfloat16)
        stores.append(pltpu.make_async_copy(ov.at[j], at_tile(out_ref, j, t), o_sems.at[j]))
        stores[-1].start()
    for copy in stores:
        copy.wait()


def weight_grad(place, pieces, arrays, xt, keep, n, width):
    depth, tokens = xt.shape
    t = tile_of(width // PARTS)
    steps = width // t
    bf16 = jnp.bfloat16
    return call(
        functools.partial(weight_grad_kernel, n, pieces, tokens ** (-0.5)),
        "weight_grad",
        place,
        [*arrays, xt, keep],
        jax.ShapeDtypeStruct((depth, width), bf16),
        [
            pltpu.VMEM((tokens, width), bf16),
            pltpu.VMEM((depth, tokens), bf16),
            pltpu.VMEM((depth // BLOCK, width), jnp.float32),
            pltpu.VMEM((steps, depth, t), bf16),
            pltpu.SemaphoreType.DMA((len(groups_of(steps)),)),
            pltpu.SemaphoreType.DMA((2,)),
            pltpu.SemaphoreType.DMA((steps,)),
        ],
    )


def finish_kernel(n, cols, links, place_ref, *refs):
    z = place_ref[0]
    each = 2 + len(links)
    sum_refs, grad_refs, (out_ref, grad_ref, sv, gv, ov, ob, sems, o_sems) = (
        refs[: each * PARTS],
        refs[each * PARTS : each * PARTS + cols],
        refs[each * PARTS + cols :],
    )
    tr, pw = sv.shape[-2:]
    for p in range(PARTS):
        for i in range(each):
            ref = sum_refs[each * p + i]
            if i < 2:
                ref = ref.at[pl.ds(pl.multiple_of(z * tr, tr), tr), :]
            pltpu.make_async_copy(ref, sv.at[p, i], sems.at[p]).start()
    for k in range(cols):
        pltpu.make_async_copy(grad_refs[k], gv.at[k], sems.at[PARTS]).start()
    odd = lax.rem(z, 2)
    stores = []
    for p in range(PARTS):
        pltpu.make_async_copy(sv.at[p], sv.at[p], sems.at[p]).wait()
        total = sv[p, 0].astype(jnp.float32) + sv[p, 1].astype(jnp.float32)
        for i, link in enumerate(links):
            other = z + 1 - 2 * odd if link == 0 else z - 1 + 2 * odd
            came = sv[p, 2 + i].astype(jnp.float32)
            total += jnp.where((other >= 0) & (other < n), came, 0.0)
        ov[p] = total.astype(jnp.bfloat16)
        stores.append(pltpu.make_async_copy(ov.at[p], out_ref.at[:, pl.ds(p * pw, pw)], o_sems.at[p]))
        stores[-1].start()
    pltpu.make_async_copy(gv, gv, sems.at[PARTS]).wait()
    total = gv[0].astype(jnp.float32)
    for k in range(1, cols):
        total += gv[k].astype(jnp.float32)
    ob[...] = total.astype(jnp.bfloat16)
    stores.append(pltpu.make_async_copy(ob, grad_ref, o_sems.at[PARTS]))
    stores[-1].start()
    for copy in stores:
        copy.wait()


def finish(place, sums, grads, links, n):
    tr, pw = sums[0][-1].shape
    rows, depth = grads[0].shape
    cols = len(grads)
    bf16 = jnp.bfloat16
    return call(
        functools.partial(finish_kernel, n, cols, links),
        "finish",
        place,
        [v for part in sums for v in part] + grads,
        [jax.ShapeDtypeStruct((tr, pw * PARTS), bf16), jax.ShapeDtypeStruct((rows, depth), bf16)],
        [
            pltpu.VMEM((PARTS, 2 + len(links), tr, pw), bf16),
            pltpu.VMEM((cols, rows, depth), bf16),
            pltpu.VMEM((PARTS, tr, pw), bf16),
            pltpu.VMEM((rows, depth), bf16),
            pltpu.SemaphoreType.DMA((PARTS + 1,)),
            pltpu.SemaphoreType.DMA((PARTS + 1,)),
        ],
    )


def local(n, cols, inputs, weight, mask, cotangent):
    row, col = lax.axis_index("row"), lax.axis_index("col")
    z, core = row // 2, row % 2
    place = jnp.stack([z, core, col]).astype(jnp.int32)
    width = weight.shape[1]
    pw = width // PARTS
    tr = cotangent.shape[0]
    tokens = tr * 2 * n

    f32, bf16 = jnp.float32, jnp.bfloat16
    swap = lambda v: lax.ppermute(v, "row", [(i, i ^ 1) for i in range(2 * n)])
    across = lambda v, k: lax.ppermute(v, "col", [(i, i ^ k) for i in range(cols)])

    def pairs_of(link, ups, downs):
        pairs = [(i, i + 1) for i in ups if i % 2 == link and i + 1 < n]
        return pairs + [(i, i - 1) for i in downs if i % 2 != link and i > 0]

    def over(v, link, ups, downs):
        pairs = pairs_of(link, ups, downs)
        if not pairs:
            return None
        pairs = [(2 * i + c, 2 * j + c) for i, j in pairs for c in range(2)]
        if {i for i, _ in pairs} == {j for _, j in pairs}:
            pairs += [(i, i ^ 1) for i in sorted(set(range(2 * n)) - {i for i, _ in pairs})]
        return lax.ppermute(v, "row", pairs)

    even = z % 2 == 0

    xs = [inputs] + [across(inputs, k) for k in range(1, cols)]
    keep = jnp.repeat(mask.astype(f32), BLOCK, axis=1)
    came = [over(cotangent, link, range(n), range(n)) for link in range(2)]
    first = came
    pieces = [((0, 0, 0), cotangent), ((0, 0, 1), swap(cotangent))]

    def keep_pieces(s):
        have = [(link, v) for link, v in enumerate(came) if v is not None]
        if len(have) == 2 and 2 * s >= n:
            origin = jnp.where(even, z + s, z - s)
            have = [(2, jnp.where((origin >= 0) & (origin < n), *came))]
        for link, v in have:
            pieces.extend([((link, s, 0), v), ((link, s, 1), swap(v))])

    keep_pieces(1)

    mine, theirs = [], []
    for p in range(PARTS):
        m, other, *more = forward(place, xs, weight, keep, first if p else (), p, n, p == 0)
        whole = more[0] if more else whole
        mine.append(m)
        theirs.append(swap(other))

    sums = [[None, None] for _ in range(PARTS)]
    sent = {}

    def slot(k, p, after):
        ups, downs = range(k - 1), range(n - k + 1, n)
        links = tuple(link for link in range(2) if pairs_of(link, ups, downs))
        sent[k, p] = send_sums(place, mine[p], theirs[p], sums[p], links, after, k, n, p == 0)
        sums[p] = [None, None]
        for link, v in zip(links, sent[k, p]):
            sums[p][link] = over(v, link, ups, downs)

    after = ()
    for k in range(2, n + 1):
        if k < n:
            came = [
                None if came[1 - link] is None else over(came[1 - link], link, range(k - 1, n), range(n - k + 1))
                for link in range(2)
            ]
        slot(k, 0, after)
        after = sent[k, 0]
        if k == 2:
            held = [(i, v) for i, v in pieces if 2 * i[1] < n]
            kinds = [i for i, _ in held]
        if k == n:
            late = [(i, v) for i, v in pieces if 2 * i[1] >= n]
            parts = late_rows(
                place, kinds, [i for i, _ in late], [v for _, v in late], weight, keep, early, after, n, cols
            )
            after = parts
        for p in range(1, PARTS):
            slot(k, p, after)
            after = sent[k, p]
        if k == 2:
            early = early_rows(place, n, kinds, [v for _, v in held], weight, keep, after)
            after = [early]
            came, after = lax.optimization_barrier((came, after))
            after = [*after, *(v for v in came if v is not None)]
        elif k < n:
            came, after = lax.optimization_barrier((came, after))
        if k < n:
            keep_pieces(k)
    xt = lax.optimization_barrier((whole, sent[3, 0]))[0].T
    grads = [parts[0]] + [across(parts[k], k) for k in range(1, cols)]
    wg = weight_grad(place, [k for k, _ in pieces], [v for _, v in pieces], xt, keep, n, width)
    links = [link for link in range(2) if sums[0][link] is not None]
    ends = [[mine[p], theirs[p], *(sums[p][link] for link in links)] for p in range(PARTS)]
    outputs, input_grad = finish(place, ends, grads, links, n)
    return outputs, input_grad, wg


def solution(mesh):
    n, cols = mesh.shape["row"] // 2, mesh.shape["col"]
    return jax.shard_map(
        functools.partial(local, n, cols),
        mesh=mesh,
        in_specs=(P("col", "row"), P("row", "col"), P("row", "col"), P("row", "col")),
        out_specs=(P("row", "col"), P("col", "row"), P("row", "col")),
        check_vma=False,
    )
```

```python
import functools

import jax
import jax.numpy as jnp
from jax import lax
from jax.experimental import pallas as pl
from jax.experimental.pallas import tpu as pltpu
from jax.sharding import PartitionSpec as P

BLOCK = 128
PARTS = 2
AHEAD = 2
ROWS_AHEAD = 4
COST = 10 ** 11
VMEM_LIMIT = 64 * 1024 * 1024


def tile_of(width):
    return next(t for t in (512, 256, 128) if width % t == 0)


def at_tile(ref, j, t):
    return ref.at[:, pl.ds(j * t, t)]


def token_places(n, cols, tokens, place_ref):
    own, tr = tokens // cols, tokens // (2 * n)
    size = min(own, tr)
    for k in range(cols):
        for i in range(own // size):
            row = (place_ref[2] ^ k) * own + i * size
            r = row // tr
            held = ((r + place_ref[1]) % 2) * (tokens // 2) + (r // 2) * tr + row % tr
            yield k, i * size, pl.multiple_of(held, size), size


def mask_tile(tile_ref, keep):
    for a in range(tile_ref.shape[0] // BLOCK):
        rows = slice(a * BLOCK, (a + 1) * BLOCK)
        tile_ref[rows, :] = tile_ref[rows, :] * keep[a : a + 1, :].astype(tile_ref.dtype)


def load_weight(w_ref, keep_ref, wv, kv, sems, part):
    steps, _, t = wv.shape
    copies = [pltpu.make_async_copy(keep_ref.at[:, pl.ds(part * steps * t, steps * t)], kv, sems.at[steps])]
    return copies + [pltpu.make_async_copy(at_tile(w_ref, part * steps + j, t), wv.at[j], sems.at[j]) for j in range(steps)]


def forward_kernel(n, cols, part, emit, place_ref, *refs):
    x_refs, (w_ref, keep_ref) = refs[:cols], refs[cols : cols + 2]
    outs, (xs, wv, kv, ov, w_sems, o_sems, x_sem) = refs[cols + 2 : -7], refs[-7:]
    steps, _, t = wv.shape
    tokens = xs.shape[0]
    half = tokens // 2
    for k, at, held, size in token_places(n, cols, tokens, place_ref):
        pltpu.make_async_copy(x_refs[k].at[pl.ds(at, size), :], xs.at[pl.ds(held, size), :], x_sem).start()
    loads = load_weight(w_ref, keep_ref, wv, kv, w_sems, part)
    for copy in loads[: 1 + AHEAD]:
        copy.start()
    pltpu.make_async_copy(xs, xs, x_sem).wait()
    stores = []
    if emit:
        stores.append(pltpu.make_async_copy(xs, outs[2], x_sem))
        stores[0].start()
    loads[0].wait()
    for j in range(steps):
        loads[1 + j].wait()
        if j + AHEAD < steps:
            loads[1 + j + AHEAD].start()
        mask_tile(wv.at[j], kv[:, j * t : (j + 1) * t])
        acc = jnp.dot(xs[...], wv[j], preferred_element_type=jnp.float32)
        ov[j] = acc.astype(jnp.bfloat16)
        for i in range(2):
            rows = pl.ds(i * half, half)
            stores.append(pltpu.make_async_copy(ov.at[j, rows, :], at_tile(outs[i], j, t), o_sems.at[i, j]))
            stores[-1].start()
    for copy in stores:
        copy.wait()


ANY = pl.BlockSpec(memory_space=pl.ANY)


def call(kernel, name, place, args, out_shape, scratch, aliases=None, after=(), cost=COST):
    held = len(args)
    body = lambda place_ref, *refs: kernel(place_ref, *refs[:held], *refs[held + len(after) :])
    return pl.pallas_call(
        body,
        grid_spec=pltpu.PrefetchScalarGridSpec(
            num_scalar_prefetch=1,
            grid=(),
            in_specs=[ANY] * (held + len(after)),
            out_specs=jax.tree.map(lambda _: ANY, out_shape),
            scratch_shapes=scratch,
        ),
        out_shape=out_shape,
        input_output_aliases=aliases or {},
        compiler_params=pltpu.CompilerParams(vmem_limit_bytes=VMEM_LIMIT),
        cost_estimate=pl.CostEstimate(flops=cost, bytes_accessed=cost, transcendentals=0),
        name=name,
    )(place, *args, *after)


def forward(place, xs, weight, keep, after, part, n, emit):
    depth, width = weight.shape
    t = tile_of(width // PARTS)
    steps = width // PARTS // t
    tokens = xs[0].shape[0] * len(xs)
    bf16 = jnp.bfloat16
    outs = [jax.ShapeDtypeStruct((tokens // 2, steps * t), bf16)] * 2
    return call(
        functools.partial(forward_kernel, n, len(xs), part, emit),
        "forward",
        place,
        [*xs, weight, keep],
        outs + ([jax.ShapeDtypeStruct((tokens, depth), bf16)] if emit else []),
        [
            pltpu.VMEM((tokens, depth), bf16),
            pltpu.VMEM((steps, depth, t), bf16),
            pltpu.VMEM((depth // BLOCK, steps * t), jnp.float32),
            pltpu.VMEM((steps, tokens, t), bf16),
            pltpu.SemaphoreType.DMA((steps + 1,)),
            pltpu.SemaphoreType.DMA((2, steps)),
            pltpu.SemaphoreType.DMA,
        ],
        after=after,
        cost=COST if part else 1,
    )


def origin_of(n, z, piece):
    link, s, _ = piece
    sign = jnp.where(z % 2 == 0, s, -s)
    if link == 2:
        return jnp.where((z + sign >= 0) & (z + sign < n), z + sign, z - sign)
    return z - sign if link == 1 else z + sign


def groups_of(steps):
    ends = sorted({min(e, steps) for e in (2, steps)})
    return list(zip([0, *ends], ends))


def start_pieces(n, place_ref, pieces, refs, held, sems, t):
    tokens, width = held.shape
    tr = tokens // (2 * n)
    for g, (lo, hi) in enumerate(groups_of(width // t)):
        for piece, ref in zip(pieces, refs):
            origin = origin_of(n, place_ref[0], piece)

            @pl.when((origin >= 0) & (origin < n))
            def _():
                at = pl.multiple_of(piece[2] * (tokens // 2) + origin * tr, tr)
                columns = pl.ds(lo * t, (hi - lo) * t)
                pltpu.make_async_copy(ref.at[:, columns], held.at[pl.ds(at, tr), columns], sems.at[g]).start()


def each_piece(n, place_ref, pieces, body):
    for i, piece in enumerate(pieces):
        origin = origin_of(n, place_ref[0], piece)
        pl.when((origin >= 0) & (origin < n))(functools.partial(body, i, origin))


def product_rows(n, place_ref, pieces, piece_refs, w_ref, keep_ref, held, wv, kv, acc, sems, w_sems):
    steps, _, t = wv.shape
    tr = held.shape[0] // len(pieces)
    loads = load_weight(w_ref, keep_ref, wv, kv, w_sems, 0)
    for copy in loads[:2]:
        copy.start()

    def rows_of(i):
        return pltpu.make_async_copy(piece_refs[i], held.at[pl.ds(i * tr, tr), :], sems.at[i])

    each_piece(n, place_ref, pieces, lambda i, _: rows_of(i).start())
    for copy in loads[2 : 1 + ROWS_AHEAD]:
        copy.start()
    each_piece(n, place_ref, pieces, lambda i, _: rows_of(i).wait())
    loads[0].wait()
    for j in range(steps):
        loads[1 + j].wait()
        if j + ROWS_AHEAD < steps:
            loads[1 + j + ROWS_AHEAD].start()
        columns = slice(j * t, (j + 1) * t)
        mask_tile(wv.at[j], kv[:, columns])
        product = lax.dot_general(held[:, columns], wv[j], (((1,), (1,)), ((), ())), preferred_element_type=jnp.float32)
        if j == 0:
            acc[...] = product
        else:
            acc[...] += product


def early_kernel(n, pieces, place_ref, *refs):
    piece_refs, (w_ref, keep_ref, out_ref, held, wv, kv, acc, ob, sems, w_sems, o_sem) = refs[: len(pieces)], refs[len(pieces) :]
    product_rows(n, place_ref, pieces, piece_refs, w_ref, keep_ref, held, wv, kv, acc, sems, w_sems)
    ob[...] = acc[...].astype(jnp.bfloat16)
    store = pltpu.make_async_copy(ob, out_ref, o_sem)
    store.start()
    store.wait()


def early_rows(place, n, pieces, arrays, weight, keep, after):
    depth, width = weight.shape
    t = tile_of(width // PARTS)
    steps = width // t
    rows = len(pieces) * arrays[0].shape[0]
    f32, bf16 = jnp.float32, jnp.bfloat16
    return call(
        functools.partial(early_kernel, n, pieces),
        "early_rows",
        place,
        [*arrays, weight, keep],
        jax.ShapeDtypeStruct((rows, depth), bf16),
        [
            pltpu.VMEM((rows, width), bf16),
            pltpu.VMEM((steps, depth, t), bf16),
            pltpu.VMEM((depth // BLOCK, width), f32),
            pltpu.VMEM((rows, depth), f32),
            pltpu.VMEM((rows, depth), bf16),
            pltpu.SemaphoreType.DMA((len(pieces),)),
            pltpu.SemaphoreType.DMA((steps + 1,)),
            pltpu.SemaphoreType.DMA,
        ],
        after=after,
    )


def late_kernel(n, cols, early, late, place_ref, *refs):
    piece_refs, (w_ref, keep_ref, early_ref), refs = refs[: len(late)], refs[len(late) : len(late) + 3], refs[len(late) + 3 :]
    out_refs, (held, wv, kv, acc, ob, sems, w_sems, e_sems, o_sem) = refs[:cols], refs[cols:]
    tokens = ob.shape[0]
    tr = tokens // (2 * n)
    rows = lambda piece, origin: pl.ds(pl.multiple_of(piece[2] * (tokens // 2) + origin * tr, tr), tr)

    def early_of(i, origin):
        return pltpu.make_async_copy(early_ref.at[pl.ds(i * tr, tr), :], ob.at[rows(early[i], origin), :], e_sems.at[i])

    each_piece(n, place_ref, early, lambda i, origin: early_of(i, origin).start())
    product_rows(n, place_ref, late, piece_refs, w_ref, keep_ref, held, wv, kv, acc, sems, w_sems)
    each_piece(n, place_ref, early, lambda i, origin: early_of(i, origin).wait())

    def store(i, origin):
        ob[rows(late[i], origin), :] = acc[i * tr : (i + 1) * tr, :].astype(jnp.bfloat16)

    each_piece(n, place_ref, late, store)
    for k, at, row, size in token_places(n, cols, tokens, place_ref):
        pltpu.make_async_copy(ob.at[pl.ds(row, size), :], out_refs[k].at[pl.ds(at, size), :], o_sem).start()
    pltpu.make_async_copy(ob, ob, o_sem).wait()


def late_rows(place, early, late, arrays, weight, keep, done, after, n, cols):
    depth, width = weight.shape
    tr = arrays[0].shape[0]
    tokens = 2 * n * tr
    t = tile_of(width // PARTS)
    steps = width // t
    f32, bf16 = jnp.float32, jnp.bfloat16
    rows = len(late) * tr
    return call(
        functools.partial(late_kernel, n, cols, early, late),
        "late_rows",
        place,
        [*arrays, weight, keep, done],
        [jax.ShapeDtypeStruct((tokens // cols, depth), bf16)] * cols,
        [
            pltpu.VMEM((rows, width), bf16),
            pltpu.VMEM((steps, depth, t), bf16),
            pltpu.VMEM((depth // BLOCK, width), f32),
            pltpu.VMEM((rows, depth), f32),
            pltpu.VMEM((tokens, depth), bf16),
            pltpu.SemaphoreType.DMA((len(late),)),
            pltpu.SemaphoreType.DMA((steps + 1,)),
            pltpu.SemaphoreType.DMA((len(early),)),
            pltpu.SemaphoreType.DMA,
        ],
        after=after,
    )


def send_kernel(n, k, links, behind, place_ref, *refs):
    mine_ref, theirs_ref, refs = refs[0], refs[1], refs[2:]
    came_refs, refs = refs[: len(behind)], refs[len(behind) :]
    out_refs, (terms, cv, ov, sems, o_sems) = refs[: len(links)], refs[len(links) :]
    tr = ov.shape[1]
    z = place_ref[0]
    odd = lax.rem(z, 2)

    def each_link(body):
        for i, link in enumerate(links):
            upward = odd == link
            d = jnp.where(upward, z + n - k + 1, z - n + k - 1)
            pl.when((d >= 0) & (d < n))(functools.partial(body, i, link, d))

    def load(i, link, d):
        for h, ref in enumerate((mine_ref, theirs_ref)):
            source = ref.at[pl.ds(pl.multiple_of(d * tr, tr), tr), :]
            pltpu.make_async_copy(source, terms.at[i, h], sems.at[i]).start()
        if 1 - link in behind:
            pltpu.make_async_copy(came_refs[behind.index(1 - link)], cv.at[i], sems.at[len(links) + i]).start()

    def add(i, link, d):
        pltpu.make_async_copy(terms.at[i], terms.at[i], sems.at[i]).wait()
        total = terms[i, 0].astype(jnp.float32) + terms[i, 1].astype(jnp.float32)
        if 1 - link in behind:
            pltpu.make_async_copy(cv.at[i], cv.at[i], sems.at[len(links) + i]).wait()
            other = z + 1 - 2 * odd if link == 1 else z - 1 + 2 * odd
            total += jnp.where((other >= 0) & (other < n), cv[i].astype(jnp.float32), 0.0)
        ov[i] = total.astype(jnp.bfloat16)
        pltpu.make_async_copy(ov.at[i], out_refs[i], o_sems.at[i]).start()

    each_link(load)
    each_link(add)
    each_link(lambda i, link, d: pltpu.make_async_copy(ov.at[i], out_refs[i], o_sems.at[i]).wait())


def send_sums(place, mine, theirs, came, links, after, k, n, first):
    behind = tuple(link for link in range(2) if came[link] is not None)
    pw = mine.shape[1]
    tr = mine.shape[0] // n
    bf16 = jnp.bfloat16
    return call(
        functools.partial(send_kernel, n, k, links, behind),
        "send_sums",
        place,
        [mine, theirs, *(came[link] for link in behind)],
        [jax.ShapeDtypeStruct((tr, pw), bf16)] * len(links),
        [
            pltpu.VMEM((len(links), 2, tr, pw), bf16),
            pltpu.VMEM((len(links), tr, pw), bf16),
            pltpu.VMEM((len(links), tr, pw), bf16),
            pltpu.SemaphoreType.DMA((2 * len(links),)),
            pltpu.SemaphoreType.DMA((len(links),)),
        ],
        after=after,
        cost=COST if k == n and first else 1,
    )


def weight_grad_kernel(n, pieces, scale, place_ref, *refs):
    piece_refs, (xt_ref, keep_ref, out_ref, held, xt, kv, ov, sems, x_sems, o_sems) = refs[: len(pieces)], refs[len(pieces) :]
    steps, _, t = ov.shape
    loads = [pltpu.make_async_copy(xt_ref, xt, x_sems.at[0]), pltpu.make_async_copy(keep_ref, kv, x_sems.at[1])]
    loads[0].start()
    start_pieces(n, place_ref, pieces, piece_refs, held, sems, t)
    loads[1].start()
    groups = groups_of(steps)
    for copy in loads:
        copy.wait()
    stores = []
    for j in range(steps):
        for g, (lo, hi) in enumerate(groups):
            if lo == j:
                part = held.at[:, pl.ds(lo * t, (hi - lo) * t)]
                pltpu.make_async_copy(part, part, sems.at[g]).wait()
        acc = jnp.dot(xt[...], held[:, j * t : (j + 1) * t], preferred_element_type=jnp.float32)
        for a in range(xt.shape[0] // BLOCK):
            rows = slice(a * BLOCK, (a + 1) * BLOCK)
            keep = kv[a : a + 1, j * t : (j + 1) * t] * scale
            ov[j, rows, :] = (acc[rows, :] * keep).astype(jnp.bfloat16)
        stores.append(pltpu.make_async_copy(ov.at[j], at_tile(out_ref, j, t), o_sems.at[j]))
        stores[-1].start()
    for copy in stores:
        copy.wait()


def weight_grad(place, pieces, arrays, xt, keep, n, width):
    depth, tokens = xt.shape
    t = tile_of(width // PARTS)
    steps = width // t
    bf16 = jnp.bfloat16
    return call(
        functools.partial(weight_grad_kernel, n, pieces, tokens ** (-0.5)),
        "weight_grad",
        place,
        [*arrays, xt, keep],
        jax.ShapeDtypeStruct((depth, width), bf16),
        [
            pltpu.VMEM((tokens, width), bf16),
            pltpu.VMEM((depth, tokens), bf16),
            pltpu.VMEM((depth // BLOCK, width), jnp.float32),
            pltpu.VMEM((steps, depth, t), bf16),
            pltpu.SemaphoreType.DMA((len(groups_of(steps)),)),
            pltpu.SemaphoreType.DMA((2,)),
            pltpu.SemaphoreType.DMA((steps,)),
        ],
    )


def finish_kernel(n, cols, links, place_ref, *refs):
    z = place_ref[0]
    each = 2 + len(links)
    sum_refs, grad_refs, (out_ref, grad_ref, sv, gv, ov, ob, sems, o_sems) = (
        refs[: each * PARTS],
        refs[each * PARTS : each * PARTS + cols],
        refs[each * PARTS + cols :],
    )
    tr, pw = sv.shape[-2:]
    for p in range(PARTS):
        for i in range(each):
            ref = sum_refs[each * p + i]
            if i < 2:
                ref = ref.at[pl.ds(pl.multiple_of(z * tr, tr), tr), :]
            pltpu.make_async_copy(ref, sv.at[p, i], sems.at[p]).start()
    for k in range(cols):
        pltpu.make_async_copy(grad_refs[k], gv.at[k], sems.at[PARTS]).start()
    odd = lax.rem(z, 2)
    stores = []
    for p in range(PARTS):
        pltpu.make_async_copy(sv.at[p], sv.at[p], sems.at[p]).wait()
        total = sv[p, 0].astype(jnp.float32) + sv[p, 1].astype(jnp.float32)
        for i, link in enumerate(links):
            other = z + 1 - 2 * odd if link == 0 else z - 1 + 2 * odd
            came = sv[p, 2 + i].astype(jnp.float32)
            total += jnp.where((other >= 0) & (other < n), came, 0.0)
        ov[p] = total.astype(jnp.bfloat16)
        stores.append(pltpu.make_async_copy(ov.at[p], out_ref.at[:, pl.ds(p * pw, pw)], o_sems.at[p]))
        stores[-1].start()
    pltpu.make_async_copy(gv, gv, sems.at[PARTS]).wait()
    total = gv[0].astype(jnp.float32)
    for k in range(1, cols):
        total += gv[k].astype(jnp.float32)
    ob[...] = total.astype(jnp.bfloat16)
    stores.append(pltpu.make_async_copy(ob, grad_ref, o_sems.at[PARTS]))
    stores[-1].start()
    for copy in stores:
        copy.wait()


def finish(place, sums, grads, links, n):
    tr, pw = sums[0][-1].shape
    rows, depth = grads[0].shape
    cols = len(grads)
    bf16 = jnp.bfloat16
    return call(
        functools.partial(finish_kernel, n, cols, links),
        "finish",
        place,
        [v for part in sums for v in part] + grads,
        [jax.ShapeDtypeStruct((tr, pw * PARTS), bf16), jax.ShapeDtypeStruct((rows, depth), bf16)],
        [
            pltpu.VMEM((PARTS, 2 + len(links), tr, pw), bf16),
            pltpu.VMEM((cols, rows, depth), bf16),
            pltpu.VMEM((PARTS, tr, pw), bf16),
            pltpu.VMEM((rows, depth), bf16),
            pltpu.SemaphoreType.DMA((PARTS + 1,)),
            pltpu.SemaphoreType.DMA((PARTS + 1,)),
        ],
    )


def local(n, cols, inputs, weight, mask, cotangent):
    row, col = lax.axis_index("row"), lax.axis_index("col")
    z, core = row // 2, row % 2
    place = jnp.stack([z, core, col]).astype(jnp.int32)
    width = weight.shape[1]
    pw = width // PARTS
    tr = cotangent.shape[0]
    tokens = tr * 2 * n

    f32, bf16 = jnp.float32, jnp.bfloat16
    swap = lambda v: lax.ppermute(v, "row", [(i, i ^ 1) for i in range(2 * n)])
    across = lambda v, k: lax.ppermute(v, "col", [(i, i ^ k) for i in range(cols)])

    def pairs_of(link, ups, downs):
        pairs = [(i, i + 1) for i in ups if i % 2 == link and i + 1 < n]
        return pairs + [(i, i - 1) for i in downs if i % 2 != link and i > 0]

    def over(v, link, ups, downs):
        pairs = pairs_of(link, ups, downs)
        if not pairs:
            return None
        pairs = [(2 * i + c, 2 * j + c) for i, j in pairs for c in range(2)]
        if {i for i, _ in pairs} == {j for _, j in pairs}:
            pairs += [(i, i ^ 1) for i in sorted(set(range(2 * n)) - {i for i, _ in pairs})]
        return lax.ppermute(v, "row", pairs)

    even = z % 2 == 0

    xs = [inputs] + [across(inputs, k) for k in range(1, cols)]
    keep = jnp.repeat(mask.astype(f32), BLOCK, axis=1)
    came = [over(cotangent, link, range(n), range(n)) for link in range(2)]
    first = came
    pieces = [((0, 0, 0), cotangent), ((0, 0, 1), swap(cotangent))]

    def keep_pieces(s):
        have = [(link, v) for link, v in enumerate(came) if v is not None]
        if len(have) == 2 and 2 * s >= n:
            origin = jnp.where(even, z + s, z - s)
            have = [(2, jnp.where((origin >= 0) & (origin < n), *came))]
        for link, v in have:
            pieces.extend([((link, s, 0), v), ((link, s, 1), swap(v))])

    keep_pieces(1)

    mine, theirs = [], []
    for p in range(PARTS):
        m, other, *more = forward(place, xs, weight, keep, first if p else (), p, n, p == 0)
        whole = more[0] if more else whole
        mine.append(m)
        theirs.append(swap(other))

    sums = [[None, None] for _ in range(PARTS)]
    sent = {}

    def slot(k, p, after):
        ups, downs = range(k - 1), range(n - k + 1, n)
        links = tuple(link for link in range(2) if pairs_of(link, ups, downs))
        sent[k, p] = send_sums(place, mine[p], theirs[p], sums[p], links, after, k, n, p == 0)
        sums[p] = [None, None]
        for link, v in zip(links, sent[k, p]):
            sums[p][link] = over(v, link, ups, downs)

    after = ()
    for k in range(2, n + 1):
        if k < n:
            came = [
                None if came[1 - link] is None else over(came[1 - link], link, range(k - 1, n), range(n - k + 1))
                for link in range(2)
            ]
        slot(k, 0, after)
        after = sent[k, 0]
        if k == 2:
            held = [(i, v) for i, v in pieces if 2 * i[1] < n]
            kinds = [i for i, _ in held]
        if k == n:
            late = [(i, v) for i, v in pieces if 2 * i[1] >= n]
            parts = late_rows(
                place, kinds, [i for i, _ in late], [v for _, v in late], weight, keep, early, after, n, cols
            )
            after = parts
        for p in range(1, PARTS):
            slot(k, p, after)
            after = sent[k, p]
        if k == 2:
            early = early_rows(place, n, kinds, [v for _, v in held], weight, keep, after)
            after = [early]
            came, after = lax.optimization_barrier((came, after))
            after = [*after, *(v for v in came if v is not None)]
        elif k < n:
            came, after = lax.optimization_barrier((came, after))
        if k < n:
            keep_pieces(k)
    xt = lax.optimization_barrier((whole, sent[3, 0]))[0].T
    grads = [parts[0]] + [across(parts[k], k) for k in range(1, cols)]
    wg = weight_grad(place, [k for k, _ in pieces], [v for _, v in pieces], xt, keep, n, width)
    links = [link for link in range(2) if sums[0][link] is not None]
    ends = [[mine[p], theirs[p], *(sums[p][link] for link in links)] for p in range(PARTS)]
    outputs, input_grad = finish(place, ends, grads, links, n)
    return outputs, input_grad, wg


def solution(mesh):
    n, cols = mesh.shape["row"] // 2, mesh.shape["col"]
    return jax.shard_map(
        functools.partial(local, n, cols),
        mesh=mesh,
        in_specs=(P("col", "row"), P("row", "col"), P("row", "col"), P("row", "col")),
        out_specs=(P("row", "col"), P("col", "row"), P("row", "col")),
        check_vma=False,
    )
```
